128 devices in a mesh: qrow: 8 (over y, x_lo), kcol: 16 (over z, x_hi, core).
Axes of the slice: x: 4 (x_hi: 2, x_lo: 2; x = x_hi * 2 + x_lo), y: 4, z: 4, core: 2. Of those that a mesh axis runs over, the one named last changes fastest.
Arguments:
- queries: bfloat16 [8192, 4096], P('qrow', 'kcol'), may hold values from -24 to 24
- key_states: bfloat16 [8192, 512], P(('kcol', 'qrow')), may hold values from -8 to 8
- value_states: bfloat16 [8192, 512], P(('kcol', 'qrow')), may hold values from -6 to 6
Outputs:
- mixed: bfloat16 [8192, 4096], P(('qrow', 'kcol'))
- log_sums: float32 [8192, 32], P(('qrow', 'kcol'))
The draws below stay inside these ranges and needn't reach their ends.
All inputs are finite; a program needn't handle non-finite values.
Results may differ from the reference program's by a relative error of at most 0.0048.
Values may be sent and summed in bfloat16 or wider, within the bound.
No kernel may reach another device: no remote copies, remote signals or barrier semaphores. Data moves between devices by JAX's collectives and lax.ppermute only.
A program may use at most 128 MiB of HBM per device.

```python
import math
import jax
import jax.numpy as jnp
from jax import lax

HQ = 32
KVH = 4
HD = 128
GROUP = 8
TOKENS = 8192
STRETCH = 1024
KB = 512
N_QROW = 8
N_KCOL = 16


def planted_row(key):
    sign_bits = jax.random.bernoulli(jax.random.fold_in(key, 11), 0.5, (KVH * HD,))
    return jnp.where(sign_bits, 8.0, -8.0).astype(jnp.float32)


def shared_keys(key, tie_factor):
    sampled = jnp.clip(jax.random.normal(key, (TOKENS, KVH * HD), jnp.float32), -8.0, 8.0)
    earlier = jnp.roll(sampled, 1, axis=0)
    odd_rows = (jnp.arange(TOKENS, dtype=jnp.int32) % 2 == 1)[:, None]
    blend_mask = jnp.where(odd_rows, tie_factor, 0.0)
    blended = sampled * (1.0 - jnp.sign(blend_mask)) + blend_mask * earlier
    final_row = (jnp.arange(TOKENS, dtype=jnp.int32) == TOKENS - 1)[:, None]
    return jnp.where(final_row, planted_row(key)[None, :], blended)


def draw_key_states(key, part):
    return shared_keys(key, 0.0).astype(jnp.bfloat16)


def draw_queries(key, part):
    key_rows = shared_keys(key, 0.0)
    key = jax.random.fold_in(key, 5)
    first_key = jax.random.fold_in(key, 0)
    gaussian = jax.random.normal(first_key, (TOKENS, HQ * HD), jnp.float32)
    row_ids = jnp.arange(TOKENS, dtype=jnp.int32)
    final_row = (row_ids == TOKENS - 1)[:, None]
    final_query = jnp.broadcast_to(key_rows[TOKENS - 1].reshape(1, KVH, 1, HD), (1, KVH, HQ // KVH, HD)).reshape(1, HQ * HD)
    final_query = 1.5 * final_query
    return jnp.clip(jnp.where(final_row, final_query, 2.0 * gaussian), -24.0, 24.0).astype(jnp.bfloat16)


def level_of(rng, shape, cuts, low, high):
    gain = 1.0
    for axis_at, shards_of in cuts:
        steps = jax.random.uniform(jax.random.fold_in(jax.random.fold_in(rng, 6), axis_at), (shards_of,), jnp.float32, low / len(cuts), high / len(cuts))
        gain = gain * jnp.repeat(jnp.exp(steps), shape[axis_at] // shards_of).reshape((-1,) + (1,) * (len(shape) - 1 - axis_at))
    return gain


def scatter_about(stream_key, extent, width, most, cuts=(), held_as=jnp.bfloat16):
    drawn = jax.random.normal(stream_key, extent, jnp.float32) * width
    if len(cuts) > 0:
        drawn = level_of(stream_key, extent, cuts, -0.22, 0.18) * drawn
    return jnp.clip(drawn, min=-most, max=most).astype(held_as)


def setup_inputs(seed: int = 0) -> dict:
    splits = jax.random.split(jax.random.key(seed), 4)
    queries = draw_queries(jax.random.fold_in(splits[3], 71), 0)
    key_states = draw_key_states(jax.random.fold_in(splits[3], 71), 0)
    value_states = scatter_about(splits[2], (TOKENS, KVH * HD), 1.0, 6.0, ((0, 128),))
    return {"queries": queries, "key_states": key_states, "value_states": value_states}


NEG_FILL = -1e+30

def block_partial(span_queries, query_pos, block_keys, block_values, key_pos):
    score_scale = 1.0 / math.sqrt(HD)
    scores = jnp.einsum('rgnd,kgd->rgnk', span_queries.astype(jnp.float32), block_keys.astype(jnp.float32)) * score_scale
    allowed = key_pos[None, None, None, :] <= query_pos[:, None, None, None]
    scores = jnp.where(allowed, scores, NEG_FILL)
    block_peak = lax.optimization_barrier(jnp.max(scores, axis=3))
    weights = jnp.where(allowed, jnp.exp(scores - block_peak[..., None]), 0.0)
    block_total = lax.optimization_barrier(jnp.sum(weights, axis=3))
    rounded_weights = lax.optimization_barrier(weights.astype(jnp.bfloat16)).astype(jnp.float32)
    numerator = jnp.einsum('rgnk,kgd->rgnd', rounded_weights, block_values.astype(jnp.float32))
    normed = (numerator / jnp.where(block_total > 0, block_total, 1.0)[..., None]).astype(jnp.bfloat16)
    row_total = span_queries.shape[0]
    return (block_peak.reshape(row_total, HQ), block_total.reshape(row_total, HQ), normed.reshape(row_total, HQ, HD))

def reference(queries, key_states, value_states):

    def one_span(span_index):
        span_queries = lax.dynamic_slice_in_dim(queries, span_index * STRETCH, STRETCH, 0).reshape(STRETCH, KVH, GROUP, HD)
        query_pos = span_index * STRETCH + jnp.arange(STRETCH, dtype=jnp.int32)

        def one_block(block_index):
            block_keys = lax.dynamic_slice_in_dim(key_states, block_index * KB, KB, 0).reshape(KB, KVH, HD)
            block_values = lax.dynamic_slice_in_dim(value_states, block_index * KB, KB, 0).reshape(KB, KVH, HD)
            key_pos = block_index * KB + jnp.arange(KB, dtype=jnp.int32)

            def compute(operand):
                return block_partial(span_queries, query_pos, block_keys, block_values, key_pos)

            def skipped(operand):
                return (jnp.full((STRETCH, HQ), NEG_FILL, jnp.float32), jnp.zeros((STRETCH, HQ), jnp.float32), jnp.zeros((STRETCH, HQ, HD), jnp.bfloat16))
            return lax.cond(block_index * KB > span_index * STRETCH + STRETCH - 1, skipped, compute, 0)
        block_peaks, block_totals, normed = lax.map(one_block, jnp.arange(N_KCOL, dtype=jnp.int32))
        run_top = lax.optimization_barrier(jnp.max(block_peaks, axis=0))
        shares = block_totals * jnp.exp(block_peaks - run_top[None])
        run_total = lax.optimization_barrier(jnp.sum(shares, axis=0))
        mixed_span = lax.optimization_barrier(jnp.sum(normed.astype(jnp.float32) * (shares / run_total[None])[..., None], axis=0))
        return (mixed_span.reshape(STRETCH, HQ * HD).astype(jnp.bfloat16), run_top + jnp.log(run_total))
    mixed_spans, log_spans = lax.map(one_span, jnp.arange(N_QROW, dtype=jnp.int32))
    return (mixed_spans.reshape(TOKENS, HQ * HD), log_spans.reshape(TOKENS, HQ))
```

```python
import math

import jax
import jax.numpy as jnp
from jax import lax
from jax.experimental import pallas as pl
from jax.experimental.pallas import tpu as pltpu
from jax.sharding import PartitionSpec as P

HQ = 32
KVH = 4
HD = 128
GROUP = 8
EVERY = ("qrow", "kcol")
SPANS = 8
SLOTS = 4
SIDES = 4

NEG_FILL = -1e30
LOG2E = math.log2(math.e)
LN2 = math.log(2.0)
WIDE = GROUP * HD + HD


def device_at(span, side, slot):
    return span * 16 + side * 4 + slot


COUPLES = [(low, SPANS - 1 - low) for low in range(SPANS // 2)]
KEY_GROUPS = [
    [
        device_at(half * 4 + near, side, xh * 2 + core)
        for side in range(SIDES)
        for xh in range(2)
        for near in range(4)
    ]
    for half in range(2)
    for core in range(2)
]
QUERY_GROUPS = [
    [device_at(span, side, slot) for span in couple for slot in range(SLOTS)]
    for couple in COUPLES
    for side in range(SIDES)
]
OUTPUT_GROUPS = [
    [device_at(span, side, slot) for span in couple for side in range(SIDES)]
    for couple in COUPLES
    for slot in range(SLOTS)
]


def attend_body(info, q_ref, first_ref, second_ref, o_ref, q_two, keys, values, acc, top):
    core, half, slot = info[2], info[3], info[4]
    tile_keys = first_ref.shape[1]
    for part, ref in enumerate((first_ref, second_ref)):
        held = slice(part * tile_keys, (part + 1) * tile_keys)
        for block in range(ref.shape[0]):
            keys[block, held, :HD] = ref[block, :, :HD]
            keys[block, held, HD:] = ref[block, :, :HD]
            values[block, held, :HD] = ref[block, :, HD:]
            values[block, held, HD:] = jnp.ones((tile_keys, HD), jnp.bfloat16)

    def step(block, tile, keep):
        rows = slice(tile * 512, (tile + 1) * 512)
        scores = lax.dot_general(
            q_two[rows, :],
            keys[block],
            (((1,), (1,)), ((), ())),
            preferred_element_type=jnp.float32,
        )
        if keep is not None:
            scores = jnp.where(keep, scores, NEG_FILL)
        old = top[rows, :]
        new = jnp.maximum(old, jnp.max(scores, axis=1, keepdims=True))
        weights = jnp.exp2(scores - new[:, 0:1])
        if keep is not None:
            weights = jnp.where(keep, weights, 0.0)
        scale = jnp.exp2(old - new)
        fresh = jnp.dot(
            weights.astype(jnp.bfloat16), values[block], preferred_element_type=jnp.float32
        )
        acc[rows, :HD] = acc[rows, :HD] * scale + fresh[:, :HD]
        acc[rows, HD:] = acc[rows, HD:] * scale + fresh[:, HD:]
        top[rows, :] = new

    lane = lax.broadcasted_iota(jnp.int32, (64, HD), 1)
    for member in range(2):
        span = info[member]
        for tile in range(4):
            for head in range(GROUP):
                piece = q_ref[
                    member * SLOTS + head // 2,
                    tile * 64 : (tile + 1) * 64,
                    (head % 2) * HD : (head % 2 + 1) * HD,
                ].astype(jnp.float32) * (LOG2E / math.sqrt(HD))
                coarse = piece.astype(jnp.bfloat16)
                at = tile * 512 + head * 64
                q_two[at : at + 64, :HD] = coarse
                q_two[at : at + 64, HD:] = (piece - coarse.astype(jnp.float32)).astype(
                    jnp.bfloat16
                )
        acc[...] = jnp.zeros_like(acc)
        top[...] = jnp.full_like(top, NEG_FILL)

        @pl.loop(0, span)
        def _(block):
            for tile in range(4):
                step(block, tile, None)

        row = lax.broadcasted_iota(jnp.int32, (512, 512), 0)
        col = lax.broadcasted_iota(jnp.int32, (512, 512), 1)
        key_at = half * 256 + jnp.where(
            col < 256, core * 512 + col, (1 - core) * 512 + col - 256
        )
        for tile in range(4):
            step(span, tile, key_at <= tile * 256 + slot * 64 + row % 64)
        for tile in range(4):
            stat = jnp.zeros((64, HD), jnp.float32)
            for head in range(GROUP):
                rows = slice(tile * 512 + head * 64, tile * 512 + head * 64 + 64)
                total = acc[rows, HD:]
                some = total > 0
                safe = jnp.where(some, total, 1.0)
                o_ref[member * 4 + tile, :, head * HD : (head + 1) * HD] = (
                    acc[rows, :HD] / safe
                ).astype(jnp.bfloat16)
                log_sum = jnp.where(some, (top[rows, :] + jnp.log2(safe)) * LN2, NEG_FILL)
                stat = jnp.where(lane % GROUP == head, log_sum, stat)
            coarse = stat.astype(jnp.bfloat16).astype(jnp.float32)
            middle = (stat - coarse).astype(jnp.bfloat16).astype(jnp.float32)
            fine = stat - coarse - middle
            o_ref[member * 4 + tile, :, GROUP * HD :] = jnp.where(
                lane < 32, coarse, jnp.where(lane < 64, middle, fine)
            ).astype(jnp.bfloat16)


def attend(info, q_pieces, first, second):
    whole = pl.BlockSpec(memory_space=pltpu.VMEM)
    return pl.pallas_call(
        attend_body,
        out_shape=jax.ShapeDtypeStruct((8, 64, WIDE), jnp.bfloat16),
        in_specs=[pl.BlockSpec(memory_space=pltpu.SMEM), whole, whole, whole],
        out_specs=whole,
        scratch_shapes=[
            pltpu.VMEM((2048, 2 * HD), jnp.bfloat16),
            pltpu.VMEM((8, 512, 2 * HD), jnp.bfloat16),
            pltpu.VMEM((8, 512, 2 * HD), jnp.bfloat16),
            pltpu.VMEM((2048, 2 * HD), jnp.float32),
            pltpu.VMEM((2048, HD), jnp.float32),
        ],
        compiler_params=pltpu.CompilerParams(vmem_limit_bytes=48 * 2**20),
        cost_estimate=pl.CostEstimate(
            flops=36 * 4 * 512 * 512 * HD,
            bytes_accessed=4 * 2**20,
            transcendentals=36 * 512 * 512,
        ),
        name="attend",
    )(info, q_pieces, first, second)


def merge_body(got_ref, mixed_ref, log_ref):
    lane = lax.broadcasted_iota(jnp.int32, (64, HD), 1)
    logs = jnp.zeros((64, HD), jnp.float32)
    for side in range(SIDES):
        sums = []
        for member in range(2):
            stat = got_ref[member * SIDES + side, :, GROUP * HD :].astype(jnp.float32)
            sums.append(stat + pltpu.roll(stat, HD - 32, 1) + pltpu.roll(stat, HD - 64, 1))
        high = jnp.maximum(sums[0], sums[1])
        joint = high + jnp.log(jnp.exp(sums[0] - high) + jnp.exp(sums[1] - high))
        logs = jnp.where(lane // GROUP == side, joint, logs)
        share = [jnp.exp(part - joint) for part in sums]
        for head in range(GROUP):
            cols = slice(head * HD, (head + 1) * HD)
            mixed_ref[:, side * GROUP * HD + head * HD : side * GROUP * HD + (head + 1) * HD] = (
                got_ref[side, :, cols].astype(jnp.float32) * share[0][:, head : head + 1]
                + got_ref[SIDES + side, :, cols].astype(jnp.float32)
                * share[1][:, head : head + 1]
            ).astype(jnp.bfloat16)
    log_ref[...] = logs[:, :HQ]


def merge(got):
    whole = pl.BlockSpec(memory_space=pltpu.VMEM)
    return pl.pallas_call(
        merge_body,
        out_shape=(
            jax.ShapeDtypeStruct((64, HQ * HD), jnp.bfloat16),
            jax.ShapeDtypeStruct((64, HQ), jnp.float32),
        ),
        in_specs=[whole],
        out_specs=(whole, whole),
        name="merge",
    )(got)


def per_device(queries, key_states, value_states):
    span = lax.axis_index("qrow")
    column = lax.axis_index("kcol")
    slot = column % 4
    core = column % 2
    half = span // 4
    low = jnp.minimum(span, SPANS - 1 - span)
    info = jnp.stack([low, SPANS - 1 - low, core, half, slot]).astype(jnp.int32)

    pieces = jnp.concatenate(
        [key_states.reshape(64, KVH, HD), value_states.reshape(64, KVH, HD)], axis=2
    ).transpose(1, 0, 2)
    pieces = jnp.broadcast_to(pieces[:, None], (KVH, 8, 64, 2 * HD)).reshape(32, 64, 2 * HD)
    own = lax.all_to_all(pieces, EVERY, 0, 0, axis_index_groups=KEY_GROUPS)
    own = own.reshape(8, 256, 2 * HD)

    sent = queries.reshape(4, SLOTS, 64, 2 * HD).transpose(1, 0, 2, 3).reshape(4, 256, 2 * HD)
    sent = jnp.concatenate([sent, sent], axis=0)
    q_pieces = lax.all_to_all(sent, EVERY, 0, 0, axis_index_groups=QUERY_GROUPS)

    other = lax.ppermute(own, EVERY, [(i, i ^ 1) for i in range(128)])
    partial = attend(info, q_pieces, own, other)
    got = lax.all_to_all(partial, EVERY, 0, 0, axis_index_groups=OUTPUT_GROUPS)
    return merge(got)


def solution(mesh):
    placed = (P("qrow", "kcol"), P(("kcol", "qrow"), None), P(("kcol", "qrow"), None))
    return jax.shard_map(
        per_device,
        mesh=mesh,
        in_specs=placed,
        out_specs=(P(("qrow", "kcol"), None), P(("qrow", "kcol"), None)),
        check_vma=False,
    )
```

```python
import functools
import math

import jax
import jax.numpy as jnp
from jax import lax
from jax.experimental import pallas as pl
from jax.experimental.pallas import tpu as pltpu
from jax.sharding import PartitionSpec as P

HQ = 32
KVH = 4
HD = 128
GROUP = 8
EVERY = ("qrow", "kcol")
SPANS = 8
DEVICES = 128
SIDES = 4

NEG_FILL = -1e30
LOG2E = math.log2(math.e)
LN2 = math.log(2.0)
HELD = 4
WIDE = HELD * HD + HD


def device_at(span, side, slot):
    return span * 16 + side * 4 + slot


KEY_GROUPS = [
    [
        device_at(half * 4 + near, side, xh * 2 + core)
        for side in range(SIDES)
        for xh in range(2)
        for near in range(4)
    ]
    for half in range(2)
    for core in range(2)
]
OUTPUT_GROUPS = [
    [
        device_at(span, side, xh * 2 + core)
        for span in (low, low ^ 6)
        for side in range(SIDES)
        for xh in range(2)
    ]
    for low in range(SPANS // 2)
    for core in range(2)
]


def pack_body(key_ref, value_ref, out_ref):
    for side in range(SIDES):
        cols = slice(side * HD, (side + 1) * HD)
        for copy in range(8):
            out_ref[side * 8 + copy, :, :HD] = key_ref[:, cols]
            out_ref[side * 8 + copy, :, HD:] = value_ref[:, cols]


def pack(key_states, value_states):
    whole = pl.BlockSpec(memory_space=pltpu.VMEM)
    return pl.pallas_call(
        pack_body,
        out_shape=jax.ShapeDtypeStruct((32, 64, 2 * HD), jnp.bfloat16),
        in_specs=[whole, whole],
        out_specs=whole,
        name="pack",
    )(key_states, value_states)


def split_body(place, q_ref, *out_refs):
    core = place[1] & 1
    for shift in range(2):
        for piece in range(8):
            at = pl.multiple_of(piece * 128 + (core ^ shift) * 64, 64)
            out_refs[shift][piece] = q_ref[pl.ds(at, 64), :]


def split(place, queries):
    whole = pl.BlockSpec(memory_space=pltpu.VMEM)
    return pl.pallas_call(
        split_body,
        out_shape=[jax.ShapeDtypeStruct((8, 64, 2 * HD), jnp.bfloat16)] * 2,
        in_specs=[pl.BlockSpec(memory_space=pltpu.SMEM), whole],
        out_specs=[whole] * 2,
        cost_estimate=pl.CostEstimate(
            flops=2 * 10**10, bytes_accessed=2**20, transcendentals=0
        ),
        name="split",
    )(place, queries)


def columns(wide):
    return [wide[:, i * HD : (i + 1) * HD] for i in range(wide.shape[1] // HD)]


def row_peak(parts):
    return jnp.max(functools.reduce(jnp.maximum, parts), axis=1, keepdims=True)


def rounded(parts):
    return jnp.concatenate([part.astype(jnp.bfloat16) for part in parts], axis=1)


def attend_body(place, *refs):
    q_refs = refs[:4]
    own_ref, other_ref, o_ref, q_all, keys, values, acc, top = refs[4:]
    row, column = place[0], place[1]
    half, core = row >> 2, column & 1

    for ref, part in ((own_ref, core), (other_ref, 1 - core)):
        held = pl.ds(pl.multiple_of(part * 256, 256), 256)
        for block in range(8):
            keys[block, held, :] = ref[block, :, :HD]
            values[block, held, :HD] = ref[block, :, HD:]
    for block in range(8):
        values[block, :, HD:] = jnp.ones((512, HD), jnp.bfloat16)

    def score(rows, block, width):
        return lax.dot_general(
            q_all[rows, :],
            keys[block, :width, :],
            (((1,), (1,)), ((), ())),
            preferred_element_type=jnp.float32,
        ) * (LOG2E / math.sqrt(HD))

    def weigh(rows, scores):
        parts = columns(scores)
        old = top[rows, :]
        new = jnp.maximum(old, row_peak(parts))
        top[rows, :] = new
        return rounded([jnp.exp2(part - new) for part in parts]), jnp.exp2(old - new)

    def add(rows, block, weights, scale):
        fresh = jnp.dot(weights, values[block], preferred_element_type=jnp.float32)
        acc[rows, :HD] = acc[rows, :HD] * scale + fresh[:, :HD]
        acc[rows, HD:] = acc[rows, HD:] * scale + fresh[:, HD:]

    tiles = [slice(tile * 512, (tile + 1) * 512) for tile in range(4)]
    lane = lax.broadcasted_iota(jnp.int32, (64, HD), 1)
    in_tile = lax.broadcasted_iota(jnp.int32, (512, HD), 0)
    in_row = (in_tile >> 8) * 128 + (in_tile & 63)
    in_col = lax.broadcasted_iota(jnp.int32, (512, HD), 1)
    for turn in range(2):
        span = row if turn == 0 else row ^ 6
        member = (row >> 2) ^ turn
        for shift in range(2):
            for piece in range(8):
                for head in range(2):
                    at = piece * 256 + (core ^ shift) * 128 + head * 64
                    q_all[pl.ds(pl.multiple_of(at, 64), 64), :] = q_refs[turn * 2 + shift][
                        piece, :, head * HD : (head + 1) * HD
                    ]

        for tile, rows in enumerate(tiles):
            width = 256 if tile < 2 else 512
            parts = columns(score(rows, span, width))
            reach = in_row + (tile % 2) * 256 + core * 64 - half * 256
            keep = [in_col + i * HD <= reach for i in range(2)]
            parts[-2:] = [jnp.where(k, p, NEG_FILL) for k, p in zip(keep, parts[-2:])]
            peak = jnp.broadcast_to(row_peak(parts), (512, HD))
            weights = [jnp.exp2(part - peak) for part in parts]
            weights[-2:] = [jnp.where(k, w, 0.0) for k, w in zip(keep, weights[-2:])]
            top[rows, :] = peak
            acc[rows, :] = jnp.dot(
                rounded(weights), values[span, :width, :], preferred_element_type=jnp.float32
            )

        @pl.loop(0, span)
        def _(block):
            ready = score(tiles[0], block, 512)
            waiting = None
            for tile, rows in enumerate(tiles):
                later = score(tiles[tile + 1], block, 512) if tile < 3 else None
                now = weigh(rows, ready)
                if waiting is not None:
                    add(tiles[tile - 1], block, *waiting)
                waiting, ready = now, later
            add(tiles[3], block, *waiting)

        for piece in range(8):
            peaks = jnp.zeros((64, HD), jnp.float32)
            totals = jnp.zeros((64, HD), jnp.float32)
            for head in range(HELD):
                at = piece * 256 + head * 64
                rows = slice(at, at + 64)
                total = acc[rows, HD:]
                o_ref[member * 8 + piece, :, head * HD : (head + 1) * HD] = (
                    acc[rows, :HD] / jnp.where(total > 0, total, 1.0)
                ).astype(jnp.bfloat16)
                mine = lane % HELD == head
                peaks = jnp.where(mine, top[rows, :], peaks)
                totals = jnp.where(mine, total, totals)
            some = totals > 0
            stat = jnp.where(
                some, (peaks + jnp.log2(jnp.where(some, totals, 1.0))) * LN2, NEG_FILL
            )
            coarse = stat.astype(jnp.bfloat16).astype(jnp.float32)
            middle = (stat - coarse).astype(jnp.bfloat16).astype(jnp.float32)
            fine = stat - coarse - middle
            o_ref[member * 8 + piece, :, HELD * HD :] = jnp.where(
                lane < 32, coarse, jnp.where(lane < 64, middle, fine)
            ).astype(jnp.bfloat16)


def attend(place, q_pieces, own, other):
    whole = pl.BlockSpec(memory_space=pltpu.VMEM)
    return pl.pallas_call(
        attend_body,
        out_shape=jax.ShapeDtypeStruct((16, 64, WIDE), jnp.bfloat16),
        in_specs=[pl.BlockSpec(memory_space=pltpu.SMEM)] + [whole] * 6,
        out_specs=whole,
        scratch_shapes=[
            pltpu.VMEM((2048, HD), jnp.bfloat16),
            pltpu.VMEM((8, 512, HD), jnp.bfloat16),
            pltpu.VMEM((8, 512, 2 * HD), jnp.bfloat16),
            pltpu.VMEM((2048, 2 * HD), jnp.float32),
            pltpu.VMEM((2048, HD), jnp.float32),
        ],
        compiler_params=pltpu.CompilerParams(vmem_limit_bytes=48 * 2**20),
        cost_estimate=pl.CostEstimate(
            flops=36 * 4 * 512 * 512 * HD,
            bytes_accessed=4 * 2**20,
            transcendentals=36 * 512 * 512,
        ),
        name="attend",
    )(place, *q_pieces, own, other)


def merge_body(got_ref, mixed_ref, log_ref):
    side = pl.program_id(0)
    lane = lax.broadcasted_iota(jnp.int32, (64, HD), 1)
    joints = []
    for xh in range(2):
        sums = []
        for member in range(2):
            stat = got_ref[member, xh, :, HELD * HD :].astype(jnp.float32)
            sums.append(stat + pltpu.roll(stat, HD - 32, 1) + pltpu.roll(stat, HD - 64, 1))
        high = jnp.maximum(sums[0], sums[1])
        joint = high + jnp.log(jnp.exp(sums[0] - high) + jnp.exp(sums[1] - high))
        joints.append(joint)
        share = [jnp.exp(part - joint) for part in sums]
        for head in range(HELD):
            cols = slice(head * HD, (head + 1) * HD)
            into = slice((xh * HELD + head) * HD, (xh * HELD + head + 1) * HD)
            mixed_ref[:, into] = (
                got_ref[0, xh, :, cols].astype(jnp.float32) * share[0][:, head : head + 1]
                + got_ref[1, xh, :, cols].astype(jnp.float32) * share[1][:, head : head + 1]
            ).astype(jnp.bfloat16)
    logs = jnp.where(lane < HELD, joints[0], joints[1])
    log_ref[pl.ds(pl.multiple_of(side * GROUP, GROUP), GROUP), :] = logs.T[:GROUP, :]


def merge(got):
    return pl.pallas_call(
        merge_body,
        grid=(SIDES,),
        out_shape=(
            jax.ShapeDtypeStruct((64, HQ * HD), jnp.bfloat16),
            jax.ShapeDtypeStruct((HQ, 64), jnp.float32),
        ),
        in_specs=[pl.BlockSpec((2, 2, 64, WIDE), lambda side: (0, side, 0, 0))],
        out_specs=(
            pl.BlockSpec((64, GROUP * HD), lambda side: (0, side)),
            pl.BlockSpec((HQ, 64), lambda side: (0, 0)),
        ),
        name="merge",
    )(got.reshape(2, 2 * SIDES, 64, WIDE))


def per_device(queries, key_states, value_states):
    row = lax.axis_index("qrow")
    column = lax.axis_index("kcol")
    place = jnp.stack([row, column])

    own = lax.all_to_all(
        pack(key_states, value_states), EVERY, 0, 0, axis_index_groups=KEY_GROUPS
    ).reshape(8, 256, 2 * HD)

    by_shift = split(place, queries)
    q_pieces = []
    for turn in range(2):
        for shift in range(2):
            piece = by_shift[shift]
            if turn or shift:
                pairs = [(i, i ^ shift ^ (96 * turn)) for i in range(DEVICES)]
                piece = lax.ppermute(piece, EVERY, pairs)
            q_pieces.append(piece)

    own, q_pieces = lax.optimization_barrier((own, q_pieces))
    other = lax.ppermute(own, EVERY, [(i, i ^ 1) for i in range(DEVICES)])
    partial = attend(place, q_pieces, own, other)
    got = lax.all_to_all(partial, EVERY, 0, 0, axis_index_groups=OUTPUT_GROUPS)
    mixed, logs = merge(got)
    return (mixed, logs.T)


def solution(mesh):
    placed = (P("qrow", "kcol"), P(("kcol", "qrow"), None), P(("kcol", "qrow"), None))
    return jax.shard_map(
        per_device,
        mesh=mesh,
        in_specs=placed,
        out_specs=(P(("qrow", "kcol"), None), P(("qrow", "kcol"), None)),
        check_vma=False,
    )
```

```python
import functools
import math

import jax
import jax.numpy as jnp
from jax import lax
from jax.experimental import pallas as pl
from jax.experimental.pallas import tpu as pltpu
from jax.sharding import PartitionSpec as P

HQ = 32
KVH = 4
HD = 128
GROUP = 8
EVERY = ("qrow", "kcol")
SPANS = 8
DEVICES = 128
SIDES = 4

NEG_FILL = -1e30
LOG2E = math.log2(math.e)
LN2 = math.log(2.0)
HELD = 4
ROWS = 72


def device_at(span, side, slot):
    return span * 16 + side * 4 + slot


KEY_GROUPS = [
    [
        device_at(half * 4 + near, side, xh * 2 + core)
        for near in range(4)
        for xh in range(2)
        for side in range(SIDES)
    ]
    for half in range(2)
    for core in range(2)
]
OUTPUT_GROUPS = [
    [
        device_at(span, side, xh * 2 + core)
        for span in (low, low ^ 6)
        for side in range(SIDES)
        for xh in range(2)
    ]
    for low in range(SPANS // 2)
    for core in range(2)
]


def pack_body(key_ref, value_ref, out_ref):
    for side in range(SIDES):
        cols = slice(side * HD, (side + 1) * HD)
        for copy in range(8):
            out_ref[copy * SIDES + side, :, :HD] = key_ref[:, cols]
            out_ref[copy * SIDES + side, :, HD:] = value_ref[:, cols]


def pack(key_states, value_states):
    whole = pl.BlockSpec(memory_space=pltpu.VMEM)
    return pl.pallas_call(
        pack_body,
        out_shape=jax.ShapeDtypeStruct((32, 64, 2 * HD), jnp.bfloat16),
        in_specs=[whole, whole],
        out_specs=whole,
        name="pack",
    )(key_states, value_states)


def split_body(place, q_ref, *out_refs):
    core = place[1] & 1
    for shift in range(2):
        for piece in range(8):
            at = pl.multiple_of(piece * 128 + (core ^ shift) * 64, 64)
            out_refs[shift][piece] = q_ref[pl.ds(at, 64), :]


def split(place, queries):
    whole = pl.BlockSpec(memory_space=pltpu.VMEM)
    return pl.pallas_call(
        split_body,
        out_shape=[jax.ShapeDtypeStruct((8, 64, 2 * HD), jnp.bfloat16)] * 2,
        in_specs=[pl.BlockSpec(memory_space=pltpu.SMEM), whole],
        out_specs=[whole] * 2,
        cost_estimate=pl.CostEstimate(
            flops=2 * 10**10, bytes_accessed=2**20, transcendentals=0
        ),
        compiler_params=pltpu.CompilerParams(vmem_limit_bytes=8 * 2**20),
        name="split",
    )(place, queries)


def columns(wide):
    return [wide[:, i * HD : (i + 1) * HD] for i in range(wide.shape[1] // HD)]


def row_peak(parts):
    return jnp.max(functools.reduce(jnp.maximum, parts), axis=1, keepdims=True)


def rounded(parts):
    return jnp.concatenate([part.astype(jnp.bfloat16) for part in parts], axis=1)


def attend_body(place, *refs):
    q_refs = refs[:4]
    own_ref, other_ref, o_ref, q_all, keys, values, acc, top = refs[4:]
    row, column = place[0], place[1]
    half, core = row >> 2, column & 1

    for ref, part in ((own_ref, core), (other_ref, 1 - core)):
        for block in range(8):
            side, xh = block // 2, block % 2
            for near in range(4):
                held = pl.ds(pl.multiple_of(part * 256 + near * 64, 64), 64)
                piece = (near * 2 + xh) * SIDES + side
                keys[block, held, :] = ref[piece, :, :HD]
                values[block, held, :HD] = ref[piece, :, HD:]
    for block in range(8):
        values[block, :, HD:] = jnp.ones((512, HD), jnp.bfloat16)

    def score(rows, block, width):
        return lax.dot_general(
            q_all[rows, :],
            keys[block, :width, :],
            (((1,), (1,)), ((), ())),
            preferred_element_type=jnp.float32,
        ) * (LOG2E / math.sqrt(HD))

    def weigh(rows, scores):
        parts = [columns(wide) for wide in scores]
        old = top[rows, :]
        new = jnp.maximum(old, row_peak(sum(parts, [])))
        top[rows, :] = new
        weights = [rounded([jnp.exp2(part - new) for part in some]) for some in parts]
        return weights, jnp.exp2(old - new)

    def add(rows, blocks, weights, scale):
        fresh = sum(
            jnp.dot(weight, values[block], preferred_element_type=jnp.float32)
            for weight, block in zip(weights, blocks)
        )
        acc[rows, :HD] = acc[rows, :HD] * scale + fresh[:, :HD]
        acc[rows, HD:] = acc[rows, HD:] * scale + fresh[:, HD:]

    tiles = [slice(tile * 512, (tile + 1) * 512) for tile in range(4)]
    lane = lax.broadcasted_iota(jnp.int32, (64, HD), 1)
    in_tile = lax.broadcasted_iota(jnp.int32, (512, HD), 0)
    in_row = (in_tile >> 8) * 128 + (in_tile & 63)
    in_col = lax.broadcasted_iota(jnp.int32, (512, HD), 1)
    for turn in range(2):
        span = row if turn == 0 else row ^ 6
        member = (row >> 2) ^ turn
        for shift in range(2):
            for piece in range(8):
                for head in range(2):
                    at = piece * 256 + (core ^ shift) * 128 + head * 64
                    q_all[pl.ds(pl.multiple_of(at, 64), 64), :] = q_refs[turn * 2 + shift][
                        piece, :, head * HD : (head + 1) * HD
                    ]

        for tile, rows in enumerate(tiles):
            width = 256 if tile < 2 else 512
            parts = columns(score(rows, span, width))
            reach = in_row + (tile % 2) * 256 + core * 64 - half * 256
            keep = [in_col + i * HD <= reach for i in range(2)]
            parts[-2:] = [jnp.where(k, p, NEG_FILL) for k, p in zip(keep, parts[-2:])]
            peak = jnp.broadcast_to(row_peak(parts), (512, HD))
            weights = [jnp.exp2(part - peak) for part in parts]
            weights[-2:] = [jnp.where(k, w, 0.0) for k, w in zip(keep, weights[-2:])]
            top[rows, :] = peak
            acc[rows, :] = jnp.dot(
                rounded(weights), values[span, :width, :], preferred_element_type=jnp.float32
            )

        def sweep(blocks):
            def ahead(tile):
                return [score(tiles[tile], block, 512) for block in blocks]

            ready, waiting = ahead(0), None
            for tile, rows in enumerate(tiles):
                later = ahead(tile + 1) if tile < 3 else None
                now = weigh(rows, ready)
                if waiting is not None:
                    add(tiles[tile - 1], blocks, *waiting)
                waiting, ready = now, later
            add(tiles[3], blocks, *waiting)

        @pl.when((span & 1) == 1)
        def _():
            sweep([span - 1])

        @pl.loop(0, span >> 1)
        def _(pair):
            sweep([pair * 2, pair * 2 + 1])

        for both in range(4):
            stats = []
            for piece in (both * 2, both * 2 + 1):
                peaks = jnp.zeros((64, HD), jnp.float32)
                totals = jnp.zeros((64, HD), jnp.float32)
                for head in range(HELD):
                    at = piece * 256 + head * 64
                    rows = slice(at, at + 64)
                    total = acc[rows, HD:]
                    o_ref[member * 8 + piece, :64, head * HD : (head + 1) * HD] = (
                        acc[rows, :HD] / jnp.where(total > 0, total, 1.0)
                    ).astype(jnp.bfloat16)
                    mine = lane % HELD == head
                    peaks = jnp.where(mine, top[rows, :], peaks)
                    totals = jnp.where(mine, total, totals)
                some = totals > 0
                stats.append(
                    jnp.where(
                        some, (peaks + jnp.log2(jnp.where(some, totals, 1.0))) * LN2, NEG_FILL
                    )
                )
            by_head = jnp.concatenate(stats, axis=0).T[:8, :]
            for part in range(2):
                stat = pltpu.roll(by_head, 64, 1) if part else by_head
                coarse = stat.astype(jnp.bfloat16).astype(jnp.float32)
                middle = (stat - coarse).astype(jnp.bfloat16).astype(jnp.float32)
                fine = stat - coarse - middle
                o_ref[member * 8 + both * 2 + part, 64:, :] = rounded(
                    [coarse, middle, fine, jnp.zeros_like(fine)]
                )


def attend(place, q_pieces, own, other):
    whole = pl.BlockSpec(memory_space=pltpu.VMEM)
    return pl.pallas_call(
        attend_body,
        out_shape=jax.ShapeDtypeStruct((16, ROWS, HELD * HD), jnp.bfloat16),
        in_specs=[pl.BlockSpec(memory_space=pltpu.SMEM)] + [whole] * 6,
        out_specs=whole,
        scratch_shapes=[
            pltpu.VMEM((2048, HD), jnp.bfloat16),
            pltpu.VMEM((8, 512, HD), jnp.bfloat16),
            pltpu.VMEM((8, 512, 2 * HD), jnp.bfloat16),
            pltpu.VMEM((2048, 2 * HD), jnp.float32),
            pltpu.VMEM((2048, HD), jnp.float32),
        ],
        compiler_params=pltpu.CompilerParams(vmem_limit_bytes=32 * 2**20),
        cost_estimate=pl.CostEstimate(
            flops=36 * 4 * 512 * 512 * HD,
            bytes_accessed=4 * 2**20,
            transcendentals=36 * 512 * 512,
        ),
        name="attend",
    )(place, *q_pieces, own, other)


def merge_body(got_ref, mixed_ref, log_ref):
    lower = lax.broadcasted_iota(jnp.int32, (8, HD), 0) < HELD
    shares = []
    for side in range(SIDES):
        joints = []
        for xh in range(2):
            sums = []
            for member in range(2):
                terms = got_ref[member, side * 2 + xh, 64:, : 3 * HD].astype(jnp.float32)
                sums.append(sum(columns(terms)))
            high = jnp.maximum(sums[0], sums[1])
            joint = high + jnp.log(jnp.exp(sums[0] - high) + jnp.exp(sums[1] - high))
            joints.append(joint)
            shares += [jnp.exp(part - joint) for part in sums]
        logs = jnp.where(lower, joints[0], joints[1])
        log_ref[side * GROUP : (side + 1) * GROUP, :] = logs[:, :64]
    share = jnp.concatenate(shares, axis=0).T[:64, :]
    for block in range(2 * SIDES):
        for head in range(HELD):
            cols = slice(head * HD, (head + 1) * HD)
            at = (block * HELD + head) * HD
            first, second = block * 16 + head, block * 16 + 8 + head
            mixed_ref[:, at : at + HD] = (
                got_ref[0, block, :64, cols].astype(jnp.float32) * share[:, first : first + 1]
                + got_ref[1, block, :64, cols].astype(jnp.float32)
                * share[:, second : second + 1]
            ).astype(jnp.bfloat16)


def merge(got):
    whole = pl.BlockSpec(memory_space=pltpu.VMEM)
    return pl.pallas_call(
        merge_body,
        out_shape=(
            jax.ShapeDtypeStruct((64, HQ * HD), jnp.bfloat16),
            jax.ShapeDtypeStruct((HQ, 64), jnp.float32),
        ),
        in_specs=[whole],
        out_specs=(whole, whole),
        compiler_params=pltpu.CompilerParams(vmem_limit_bytes=8 * 2**20),
        name="merge",
    )(got.reshape(2, 2 * SIDES, ROWS, HELD * HD))


def per_device(queries, key_states, value_states):
    row = lax.axis_index("qrow")
    column = lax.axis_index("kcol")
    place = jnp.stack([row, column])

    own = lax.all_to_all(
        pack(key_states, value_states), EVERY, 0, 0, axis_index_groups=KEY_GROUPS
    )

    by_shift = split(place, queries)
    q_pieces = []
    for turn in range(2):
        for shift in range(2):
            piece = by_shift[shift]
            if turn or shift:
                pairs = [(i, i ^ shift ^ (96 * turn)) for i in range(DEVICES)]
                piece = lax.ppermute(piece, EVERY, pairs)
            q_pieces.append(piece)

    own, q_pieces[1:] = lax.optimization_barrier((own, q_pieces[1:]))
    other = lax.ppermute(own, EVERY, [(i, i ^ 1) for i in range(DEVICES)])
    partial = attend(place, q_pieces, own, other)
    got = lax.all_to_all(partial, EVERY, 0, 0, axis_index_groups=OUTPUT_GROUPS)
    mixed, logs = merge(got)
    return (mixed, logs.T)


def solution(mesh):
    placed = (P("qrow", "kcol"), P(("kcol", "qrow"), None), P(("kcol", "qrow"), None))
    return jax.shard_map(
        per_device,
        mesh=mesh,
        in_specs=placed,
        out_specs=(P(("qrow", "kcol"), None), P(("qrow", "kcol"), None)),
        check_vma=False,
    )
```

```python
import functools
import math

import jax
import jax.numpy as jnp
from jax import lax
from jax.experimental import pallas as pl
from jax.experimental.pallas import tpu as pltpu
from jax.sharding import PartitionSpec as P

HQ = 32
KVH = 4
HD = 128
GROUP = 8
EVERY = ("qrow", "kcol")
SPANS = 8
DEVICES = 128
SIDES = 4

NEG_FILL = -1e30
LOG2E = math.log2(math.e)
LN2 = math.log(2.0)
HELD = 4
DEPTH = 136


def device_at(span, side, slot):
    return span * 16 + side * 4 + slot


KEY_GROUPS = [
    [
        device_at(half * 4 + near, side, xh * 2 + core)
        for near in range(4)
        for xh in range(2)
        for side in range(SIDES)
    ]
    for half in range(2)
    for core in range(2)
]
OUTPUT_GROUPS = [
    [
        device_at(span, side, xh * 2 + core)
        for span in (low, low ^ 6)
        for side in range(SIDES)
        for xh in range(2)
    ]
    for low in range(SPANS // 2)
    for core in range(2)
]


def pack_body(key_ref, value_ref, out_ref):
    for side in range(SIDES):
        cols = slice(side * HD, (side + 1) * HD)
        for copy in range(8):
            out_ref[copy * SIDES + side, :, :HD] = key_ref[:, cols]
            out_ref[copy * SIDES + side, :, HD:] = value_ref[:, cols]


def pack(key_states, value_states):
    whole = pl.BlockSpec(memory_space=pltpu.VMEM)
    return pl.pallas_call(
        pack_body,
        out_shape=jax.ShapeDtypeStruct((32, 64, 2 * HD), jnp.bfloat16),
        in_specs=[whole, whole],
        out_specs=whole,
        name="pack",
    )(key_states, value_states)


def split_body(place, q_ref, *out_refs):
    core = place[1] & 1
    for shift in range(2):
        for piece in range(8):
            at = pl.multiple_of(piece * 128 + (core ^ shift) * 64, 64)
            out_refs[shift][piece] = q_ref[pl.ds(at, 64), :]


def split(place, queries):
    whole = pl.BlockSpec(memory_space=pltpu.VMEM)
    return pl.pallas_call(
        split_body,
        out_shape=[jax.ShapeDtypeStruct((8, 64, 2 * HD), jnp.bfloat16)] * 2,
        in_specs=[pl.BlockSpec(memory_space=pltpu.SMEM), whole],
        out_specs=[whole] * 2,
        cost_estimate=pl.CostEstimate(
            flops=2 * 10**10, bytes_accessed=2**20, transcendentals=0
        ),
        compiler_params=pltpu.CompilerParams(vmem_limit_bytes=8 * 2**20),
        name="split",
    )(place, queries)


def grouped(scores):
    return scores.reshape(scores.shape[0] // 8, 8, scores.shape[1])


def highest(parts):
    high = functools.reduce(jnp.maximum, [jnp.max(grouped(part), axis=0) for part in parts])
    return jnp.broadcast_to(jnp.max(high, axis=0, keepdims=True), high.shape)


def exponentials(parts, peak):
    return [
        jnp.exp2(grouped(part) - peak[None]).reshape(part.shape) for part in parts
    ]


def summed(parts):
    return functools.reduce(jnp.add, [jnp.sum(grouped(part), axis=0) for part in parts])


def attend_body(place, *refs):
    q_refs = refs[:4]
    own_ref, other_ref, o_ref, q_all, keys, values, acc, top, total, key_size, safe_now = refs[4:]
    row, column = place[0], place[1]
    half, core = row >> 2, column & 1

    for ref, part in ((own_ref, core), (other_ref, 1 - core)):
        for block in range(8):
            side, xh = block // 2, block % 2
            for near in range(4):
                held = pl.ds(pl.multiple_of(part * 256 + near * 64, 64), 64)
                piece = (near * 2 + xh) * SIDES + side
                keys[block, held, :] = ref[piece, :, :HD]
                values[block, held, :] = ref[piece, :, HD:]

    def lengths(vectors):
        return lax.dot_general(
            jnp.ones((8, HD), jnp.bfloat16),
            vectors * vectors,
            (((1,), (1,)), ((), ())),
            preferred_element_type=jnp.float32,
        )

    for block in range(7):
        key_size[block] = lengths(keys[block])

    def score(tile, block, width):
        return lax.dot_general(
            keys[block, :width, :],
            q_all[tile * 512 : (tile + 1) * 512, :],
            (((1,), (1,)), ((), ())),
            preferred_element_type=jnp.float32,
        ) * (LOG2E / math.sqrt(HD))

    def gathered(blocks, weights):
        return sum(
            lax.dot_general(
                values[block, : weight.shape[0], :],
                weight.astype(jnp.bfloat16),
                (((0,), (0,)), ((), ())),
                preferred_element_type=jnp.float32,
            )
            for block, weight in zip(blocks, weights)
        )

    def weigh(tile, parts):
        old = top[tile]
        new = jnp.maximum(old, highest(parts))
        scale = jnp.exp2(old - new)
        weights = exponentials(parts, new)
        top[tile] = new
        total[tile] = total[tile] * scale + summed(weights)
        return weights, scale

    def add(tile, blocks, weights, scale):
        acc[tile] = acc[tile] * scale[:1] + gathered(blocks, weights)

    in_key = lax.broadcasted_iota(jnp.int32, (256, 512), 0)
    in_tile = lax.broadcasted_iota(jnp.int32, (256, 512), 1)
    in_row = (in_tile >> 8) * 128 + (in_tile & 63)
    for turn in range(2):
        span = row if turn == 0 else row ^ 6
        member = (row >> 2) ^ turn
        for shift in range(2):
            for piece in range(8):
                for head in range(2):
                    at = piece * 256 + (core ^ shift) * 128 + head * 64
                    q_all[pl.ds(pl.multiple_of(at, 64), 64), :] = q_refs[turn * 2 + shift][
                        piece, :, head * HD : (head + 1) * HD
                    ]

        def ahead(tile):
            return score(tile, span, 256 if tile < 2 else 512)

        ready = ahead(0)
        for tile in range(4):
            later = ahead(tile + 1) if tile < 3 else None
            edge, parts = ready[-256:], [ready[:256]] if tile >= 2 else []
            reach = in_row + (tile % 2) * 256 + core * 64 - half * 256
            keep = in_key <= reach
            edge = jnp.where(keep, edge, NEG_FILL)
            peak = highest(parts + [edge])
            weights = exponentials(parts, peak)
            weights.append(jnp.where(keep, exponentials([edge], peak)[0], 0.0))
            top[tile] = peak
            total[tile] = summed(weights)
            acc[tile] = gathered([span], [jnp.concatenate(weights, axis=0)])
            ready = later

        longest = jnp.zeros((8, 512), jnp.float32)
        for block in range(7):
            longest = jnp.maximum(longest, jnp.where(block < span, key_size[block], 0.0))
        longest = jnp.max(longest)

        def settle():
            over, held = [], []
            for tile in range(4):
                squares = lengths(q_all[tile * 512 : (tile + 1) * 512, :])
                bound = jnp.sqrt(squares * longest) * (1.02 * LOG2E / math.sqrt(HD))
                held.append(jnp.where(top[tile] > 0.5 * NEG_FILL, top[tile], 0.0))
                over.append(bound - held[tile])
            calm = jnp.max(functools.reduce(jnp.maximum, over)) <= 100.0
            safe_now[0] = calm.astype(jnp.int32)

            @pl.when(calm)
            def _():
                for tile in range(4):
                    top[tile] = held[tile]

        settle()

        def sweep(blocks):
            units = [(tile, block, at) for block in blocks for tile in range(4) for at in range(0, 512, 512)]

            def unit_score(unit):
                tile, block, at = unit
                return lax.dot_general(
                    keys[block, at : at + 512, :],
                    q_all[tile * 512 : (tile + 1) * 512, :],
                    (((1,), (1,)), ((), ())),
                    preferred_element_type=jnp.float32,
                ) * (LOG2E / math.sqrt(HD))

            def unit_add(unit, weight):
                tile, block, at = unit
                acc[tile] += lax.dot_general(
                    values[block, at : at + 512, :],
                    weight,
                    (((0,), (0,)), ((), ())),
                    preferred_element_type=jnp.float32,
                )

            ready, waiting = unit_score(units[0]), None
            for index, unit in enumerate(units):
                later = unit_score(units[index + 1]) if index + 1 < len(units) else None
                weight = exponentials([ready], top[unit[0]])[0]
                total[unit[0]] += summed([weight])
                if waiting is not None:
                    unit_add(units[index - 1], waiting)
                waiting, ready = weight.astype(jnp.bfloat16), later
            unit_add(units[-1], waiting)

        def exact_sweep(block):
            for tile in range(4):
                weights, scale = weigh(tile, [score(tile, block, 512)])
                add(tile, [block], weights, scale)

        @pl.loop(0, span // 2)
        def _(group):
            calm = safe_now[0]

            @pl.when(calm == 1)
            def _():
                sweep([group * 2 + i for i in range(2)])

            @pl.when(calm == 0)
            def _():
                for i in range(2):
                    exact_sweep(group * 2 + i)
                settle()

        @pl.when((span & 1) == 1)
        def _():
            calm = safe_now[0]

            @pl.when(calm == 1)
            def _():
                sweep([span - 1])

            @pl.when(calm == 0)
            def _():
                exact_sweep(span - 1)

        term = lax.broadcasted_iota(jnp.int32, (8, 512), 0)
        for tile in range(4):
            whole = jnp.sum(total[tile], axis=0, keepdims=True)
            some = whole > 0
            safe = jnp.where(some, whole, 1.0)
            normed = (acc[tile] * (1.0 / safe)).astype(jnp.bfloat16)
            stat = jnp.where(some, (top[tile] + jnp.log2(safe)) * LN2, NEG_FILL)
            coarse = stat.astype(jnp.bfloat16).astype(jnp.float32)
            middle = (stat - coarse).astype(jnp.bfloat16).astype(jnp.float32)
            fine = stat - coarse - middle
            terms = jnp.where(term == 0, coarse, jnp.where(term == 1, middle, fine))
            for part in range(2):
                cols = slice(part * 256, (part + 1) * 256)
                at = member * 8 + tile * 2 + part
                o_ref[at, :HD, :] = normed[:, cols]
                o_ref[at, HD:, :] = terms[:, cols].astype(jnp.bfloat16)


def attend(place, q_pieces, own, other):
    whole = pl.BlockSpec(memory_space=pltpu.VMEM)
    return pl.pallas_call(
        attend_body,
        out_shape=jax.ShapeDtypeStruct((16, DEPTH, 256), jnp.bfloat16),
        in_specs=[pl.BlockSpec(memory_space=pltpu.SMEM)] + [whole] * 6,
        out_specs=whole,
        scratch_shapes=[
            pltpu.VMEM((2048, HD), jnp.bfloat16),
            pltpu.VMEM((8, 512, HD), jnp.bfloat16),
            pltpu.VMEM((8, 512, HD), jnp.bfloat16),
            pltpu.VMEM((4, HD, 512), jnp.float32),
            pltpu.VMEM((4, 8, 512), jnp.float32),
            pltpu.VMEM((4, 8, 512), jnp.float32),
            pltpu.VMEM((7, 8, 512), jnp.float32),
            pltpu.SMEM((1,), jnp.int32),
        ],
        compiler_params=pltpu.CompilerParams(vmem_limit_bytes=32 * 2**20),
        cost_estimate=pl.CostEstimate(
            flops=36 * 4 * 512 * 512 * HD,
            bytes_accessed=4 * 2**20,
            transcendentals=36 * 512 * 512,
        ),
        name="attend",
    )(place, *q_pieces, own, other)


def merge_body(got_ref, mixed_ref, log_ref):
    for block in range(2 * SIDES):
        sums = []
        for member in range(2):
            terms = got_ref[member, block, HD:, :].astype(jnp.float32)
            sums.append(terms[0:1] + terms[1:2] + terms[2:3])
        high = jnp.maximum(sums[0], sums[1])
        joint = high + jnp.log(jnp.exp(sums[0] - high) + jnp.exp(sums[1] - high))
        mixed = got_ref[0, block, :HD, :].astype(jnp.float32) * jnp.exp(sums[0] - joint) + (
            got_ref[1, block, :HD, :].astype(jnp.float32) * jnp.exp(sums[1] - joint)
        )
        for pair in range(2):
            rows = mixed[:, pair * HD : (pair + 1) * HD].T.astype(jnp.bfloat16)
            for head in range(2):
                place = block * HELD + pair * 2 + head
                mixed_ref[:, place * HD : (place + 1) * HD] = rows[head * 64 : (head + 1) * 64]
                at = (pair * 2 + head) * 64
                log_ref[place : place + 1, :] = joint[:, at : at + 64]


def merge(got):
    whole = pl.BlockSpec(memory_space=pltpu.VMEM)
    return pl.pallas_call(
        merge_body,
        out_shape=(
            jax.ShapeDtypeStruct((64, HQ * HD), jnp.bfloat16),
            jax.ShapeDtypeStruct((HQ, 64), jnp.float32),
        ),
        in_specs=[whole],
        out_specs=(whole, whole),
        compiler_params=pltpu.CompilerParams(vmem_limit_bytes=8 * 2**20),
        name="merge",
    )(got.reshape(2, 2 * SIDES, DEPTH, 256))


def per_device(queries, key_states, value_states):
    row = lax.axis_index("qrow")
    column = lax.axis_index("kcol")
    place = jnp.stack([row, column])

    own = lax.all_to_all(
        pack(key_states, value_states), EVERY, 0, 0, axis_index_groups=KEY_GROUPS
    )

    by_shift = split(place, queries)
    q_pieces = []
    for turn in range(2):
        for shift in range(2):
            piece = by_shift[shift]
            if turn or shift:
                pairs = [(i, i ^ shift ^ (96 * turn)) for i in range(DEVICES)]
                piece = lax.ppermute(piece, EVERY, pairs)
            q_pieces.append(piece)

    own, q_pieces[1:] = lax.optimization_barrier((own, q_pieces[1:]))
    other = lax.ppermute(own, EVERY, [(i, i ^ 1) for i in range(DEVICES)])
    partial = attend(place, q_pieces, own, other)
    got = lax.all_to_all(partial, EVERY, 0, 0, axis_index_groups=OUTPUT_GROUPS)
    mixed, logs = merge(got)
    return (mixed, logs.T)


def solution(mesh):
    placed = (P("qrow", "kcol"), P(("kcol", "qrow"), None), P(("kcol", "qrow"), None))
    return jax.shard_map(
        per_device,
        mesh=mesh,
        in_specs=placed,
        out_specs=(P(("qrow", "kcol"), None), P(("qrow", "kcol"), None)),
        check_vma=False,
    )
```

```python
import functools
import math

import jax
import jax.numpy as jnp
from jax import lax
from jax.experimental import pallas as pl
from jax.experimental.pallas import tpu as pltpu
from jax.sharding import PartitionSpec as P

HQ = 32
KVH = 4
HD = 128
GROUP = 8
EVERY = ("qrow", "kcol")
SPANS = 8
DEVICES = 128
SIDES = 4

NEG_FILL = -1e30
LOG2E = math.log2(math.e)
LN2 = math.log(2.0)
HELD = 4
DEPTH = 136


def device_at(span, side, slot):
    return span * 16 + side * 4 + slot


KEY_GROUPS = [
    [
        device_at(half * 4 + near, side, xh * 2 + core)
        for near in range(4)
        for xh in range(2)
        for side in range(SIDES)
    ]
    for half in range(2)
    for core in range(2)
]
OUTPUT_GROUPS = [
    [
        device_at(span, side, xh * 2 + core)
        for span in (low, low ^ 6)
        for side in range(SIDES)
        for xh in range(2)
    ]
    for low in range(SPANS // 2)
    for core in range(2)
]


def pack_body(key_ref, value_ref, out_ref):
    for side in range(SIDES):
        cols = slice(side * HD, (side + 1) * HD)
        for copy in range(8):
            out_ref[copy * SIDES + side, :, :HD] = key_ref[:, cols]
            out_ref[copy * SIDES + side, :, HD:] = value_ref[:, cols]


def pack(key_states, value_states):
    whole = pl.BlockSpec(memory_space=pltpu.VMEM)
    return pl.pallas_call(
        pack_body,
        out_shape=jax.ShapeDtypeStruct((32, 64, 2 * HD), jnp.bfloat16),
        in_specs=[whole, whole],
        out_specs=whole,
        name="pack",
    )(key_states, value_states)


def split_body(place, q_ref, *out_refs):
    core = place[1] & 1
    for shift in range(2):
        for piece in range(8):
            at = pl.multiple_of(piece * 128 + (core ^ shift) * 64, 64)
            out_refs[shift][piece] = q_ref[pl.ds(at, 64), :]


def split(place, queries):
    whole = pl.BlockSpec(memory_space=pltpu.VMEM)
    return pl.pallas_call(
        split_body,
        out_shape=[jax.ShapeDtypeStruct((8, 64, 2 * HD), jnp.bfloat16)] * 2,
        in_specs=[pl.BlockSpec(memory_space=pltpu.SMEM), whole],
        out_specs=[whole] * 2,
        cost_estimate=pl.CostEstimate(
            flops=2 * 10**10, bytes_accessed=2**20, transcendentals=0
        ),
        compiler_params=pltpu.CompilerParams(vmem_limit_bytes=8 * 2**20),
        name="split",
    )(place, queries)


def grouped(scores):
    return scores.reshape(scores.shape[0] // 8, 8, scores.shape[1])


def highest(parts):
    high = functools.reduce(jnp.maximum, [jnp.max(grouped(part), axis=0) for part in parts])
    return jnp.broadcast_to(jnp.max(high, axis=0, keepdims=True), high.shape)


def exponentials(parts, peak):
    return [
        jnp.exp2(grouped(part) - peak[None]).reshape(part.shape) for part in parts
    ]


def summed(parts):
    return functools.reduce(jnp.add, [jnp.sum(grouped(part), axis=0) for part in parts])


def attend_body(place, *refs):
    q_refs = refs[:4]
    own_ref, other_ref, o_ref, q_all, keys, values, acc, top, total, key_size, safe_now = refs[4:]
    row, column = place[0], place[1]
    half, core = row >> 2, column & 1

    for ref, part in ((own_ref, core), (other_ref, 1 - core)):
        for block in range(8):
            side, xh = block // 2, block % 2
            for near in range(4):
                held = pl.ds(pl.multiple_of(part * 256 + near * 64, 64), 64)
                piece = (near * 2 + xh) * SIDES + side
                keys[block, held, :] = ref[piece, :, :HD]
                values[block, held, :] = ref[piece, :, HD:]

    def lengths(vectors):
        return lax.dot_general(
            jnp.ones((8, HD), jnp.bfloat16),
            vectors * vectors,
            (((1,), (1,)), ((), ())),
            preferred_element_type=jnp.float32,
        )

    for block in range(7):
        key_size[block] = lengths(keys[block])

    def score(tile, block, width):
        return lax.dot_general(
            keys[block, :width, :],
            q_all[tile * 512 : (tile + 1) * 512, :],
            (((1,), (1,)), ((), ())),
            preferred_element_type=jnp.float32,
        ) * (LOG2E / math.sqrt(HD))

    def gathered(blocks, weights):
        return sum(
            lax.dot_general(
                values[block, : weight.shape[0], :],
                weight.astype(jnp.bfloat16),
                (((0,), (0,)), ((), ())),
                preferred_element_type=jnp.float32,
            )
            for block, weight in zip(blocks, weights)
        )

    def weigh(tile, parts):
        old = top[tile]
        new = jnp.maximum(old, highest(parts))
        scale = jnp.exp2(old - new)
        weights = exponentials(parts, new)
        top[tile] = new
        total[tile] = total[tile] * scale + summed(weights)
        return weights, scale

    def add(tile, blocks, weights, scale):
        acc[tile] = acc[tile] * scale[:1] + gathered(blocks, weights)

    in_key = lax.broadcasted_iota(jnp.int32, (256, 512), 0)
    in_tile = lax.broadcasted_iota(jnp.int32, (256, 512), 1)
    in_row = (in_tile >> 8) * 128 + (in_tile & 63)
    for turn in range(2):
        span = row if turn == 0 else row ^ 6
        member = (row >> 2) ^ turn
        for shift in range(2):
            for piece in range(8):
                for head in range(2):
                    at = piece * 256 + (core ^ shift) * 128 + head * 64
                    q_all[pl.ds(pl.multiple_of(at, 64), 64), :] = q_refs[turn * 2 + shift][
                        piece, :, head * HD : (head + 1) * HD
                    ]

        def ahead(tile):
            return score(tile, span, 256 if tile < 2 else 512)

        ready = ahead(0)
        for tile in range(4):
            later = ahead(tile + 1) if tile < 3 else None
            edge, parts = ready[-256:], [ready[:256]] if tile >= 2 else []
            reach = in_row + (tile % 2) * 256 + core * 64 - half * 256
            keep = in_key <= reach
            edge = jnp.where(keep, edge, NEG_FILL)
            peak = highest(parts + [edge])
            weights = exponentials(parts, peak)
            weights.append(jnp.where(keep, exponentials([edge], peak)[0], 0.0))
            top[tile] = peak
            total[tile] = summed(weights)
            acc[tile] = gathered([span], [jnp.concatenate(weights, axis=0)])
            ready = later

        longest = jnp.zeros((8, 512), jnp.float32)
        for block in range(7):
            longest = jnp.maximum(longest, jnp.where(block < span, key_size[block], 0.0))
        longest = jnp.max(longest)

        def settle():
            fixed, width, lift = [], [], []
            for tile in range(4):
                squares = lengths(q_all[tile * 512 : (tile + 1) * 512, :])
                bound = jnp.sqrt(squares * longest) * (1.004 * LOG2E / math.sqrt(HD))
                some = top[tile] > 0.5 * NEG_FILL
                low = jnp.where(some, top[tile], -bound)
                fixed.append(jnp.maximum(low, bound - 112.0))
                width.append(bound - low)
                lift.append(jnp.where(some, fixed[tile] - low, 0.0))
            calm = jnp.max(functools.reduce(jnp.maximum, width)) <= 212.0
            lifted = jnp.max(functools.reduce(jnp.maximum, lift)) > 0.0
            safe_now[0] = calm.astype(jnp.int32)

            @pl.when(jnp.logical_and(calm, lifted))
            def _():
                for tile in range(4):
                    scale = jnp.exp2(top[tile] - fixed[tile])
                    total[tile] = total[tile] * scale
                    acc[tile] = acc[tile] * scale[:1]

            @pl.when(calm)
            def _():
                for tile in range(4):
                    top[tile] = fixed[tile]

        settle()

        def sweep(blocks):
            units = [(tile, block, at) for block in blocks for tile in range(4) for at in range(0, 512, 512)]

            def unit_score(unit):
                tile, block, at = unit
                return lax.dot_general(
                    keys[block, at : at + 512, :],
                    q_all[tile * 512 : (tile + 1) * 512, :],
                    (((1,), (1,)), ((), ())),
                    preferred_element_type=jnp.float32,
                ) * (LOG2E / math.sqrt(HD))

            def unit_add(unit, weight):
                tile, block, at = unit
                acc[tile] += lax.dot_general(
                    values[block, at : at + 512, :],
                    weight,
                    (((0,), (0,)), ((), ())),
                    preferred_element_type=jnp.float32,
                )

            ready, waiting = unit_score(units[0]), None
            for index, unit in enumerate(units):
                later = unit_score(units[index + 1]) if index + 1 < len(units) else None
                weight = exponentials([ready], top[unit[0]])[0]
                total[unit[0]] += summed([weight])
                if waiting is not None:
                    unit_add(units[index - 1], waiting)
                waiting, ready = weight.astype(jnp.bfloat16), later
            unit_add(units[-1], waiting)

        def exact_sweep(block):
            for tile in range(4):
                weights, scale = weigh(tile, [score(tile, block, 512)])
                add(tile, [block], weights, scale)

        @pl.loop(0, span // 2)
        def _(group):
            calm = safe_now[0]

            @pl.when(calm == 1)
            def _():
                sweep([group * 2 + i for i in range(2)])

            @pl.when(calm == 0)
            def _():
                for i in range(2):
                    exact_sweep(group * 2 + i)
                settle()

        @pl.when((span & 1) == 1)
        def _():
            calm = safe_now[0]

            @pl.when(calm == 1)
            def _():
                sweep([span - 1])

            @pl.when(calm == 0)
            def _():
                exact_sweep(span - 1)

        term = lax.broadcasted_iota(jnp.int32, (8, 512), 0)
        for tile in range(4):
            whole = jnp.sum(total[tile], axis=0, keepdims=True)
            some = whole > 0
            safe = jnp.where(some, whole, 1.0)
            normed = (acc[tile] * (1.0 / safe)).astype(jnp.bfloat16)
            stat = jnp.where(some, (top[tile] + jnp.log2(safe)) * LN2, NEG_FILL)
            coarse = stat.astype(jnp.bfloat16).astype(jnp.float32)
            middle = (stat - coarse).astype(jnp.bfloat16).astype(jnp.float32)
            fine = stat - coarse - middle
            terms = jnp.where(term == 0, coarse, jnp.where(term == 1, middle, fine))
            for part in range(2):
                cols = slice(part * 256, (part + 1) * 256)
                at = member * 8 + tile * 2 + part
                o_ref[at, :HD, :] = normed[:, cols]
                o_ref[at, HD:, :] = terms[:, cols].astype(jnp.bfloat16)


def attend(place, q_pieces, own, other):
    whole = pl.BlockSpec(memory_space=pltpu.VMEM)
    return pl.pallas_call(
        attend_body,
        out_shape=jax.ShapeDtypeStruct((16, DEPTH, 256), jnp.bfloat16),
        in_specs=[pl.BlockSpec(memory_space=pltpu.SMEM)] + [whole] * 6,
        out_specs=whole,
        scratch_shapes=[
            pltpu.VMEM((2048, HD), jnp.bfloat16),
            pltpu.VMEM((8, 512, HD), jnp.bfloat16),
            pltpu.VMEM((8, 512, HD), jnp.bfloat16),
            pltpu.VMEM((4, HD, 512), jnp.float32),
            pltpu.VMEM((4, 8, 512), jnp.float32),
            pltpu.VMEM((4, 8, 512), jnp.float32),
            pltpu.VMEM((7, 8, 512), jnp.float32),
            pltpu.SMEM((1,), jnp.int32),
        ],
        compiler_params=pltpu.CompilerParams(vmem_limit_bytes=32 * 2**20),
        cost_estimate=pl.CostEstimate(
            flops=36 * 4 * 512 * 512 * HD,
            bytes_accessed=4 * 2**20,
            transcendentals=36 * 512 * 512,
        ),
        name="attend",
    )(place, *q_pieces, own, other)


def merge_body(got_ref, mixed_ref, log_ref):
    for block in range(2 * SIDES):
        sums = []
        for member in range(2):
            terms = got_ref[member, block, HD:, :].astype(jnp.float32)
            sums.append(terms[0:1] + terms[1:2] + terms[2:3])
        high = jnp.maximum(sums[0], sums[1])
        joint = high + jnp.log(jnp.exp(sums[0] - high) + jnp.exp(sums[1] - high))
        mixed = got_ref[0, block, :HD, :].astype(jnp.float32) * jnp.exp(sums[0] - joint) + (
            got_ref[1, block, :HD, :].astype(jnp.float32) * jnp.exp(sums[1] - joint)
        )
        for pair in range(2):
            rows = mixed[:, pair * HD : (pair + 1) * HD].T.astype(jnp.bfloat16)
            for head in range(2):
                place = block * HELD + pair * 2 + head
                mixed_ref[:, place * HD : (place + 1) * HD] = rows[head * 64 : (head + 1) * 64]
                at = (pair * 2 + head) * 64
                log_ref[place : place + 1, :] = joint[:, at : at + 64]


def merge(got):
    whole = pl.BlockSpec(memory_space=pltpu.VMEM)
    return pl.pallas_call(
        merge_body,
        out_shape=(
            jax.ShapeDtypeStruct((64, HQ * HD), jnp.bfloat16),
            jax.ShapeDtypeStruct((HQ, 64), jnp.float32),
        ),
        in_specs=[whole],
        out_specs=(whole, whole),
        compiler_params=pltpu.CompilerParams(vmem_limit_bytes=8 * 2**20),
        name="merge",
    )(got.reshape(2, 2 * SIDES, DEPTH, 256))


def per_device(queries, key_states, value_states):
    row = lax.axis_index("qrow")
    column = lax.axis_index("kcol")
    place = jnp.stack([row, column])

    own = lax.all_to_all(
        pack(key_states, value_states), EVERY, 0, 0, axis_index_groups=KEY_GROUPS
    )

    by_shift = split(place, queries)
    q_pieces = []
    for turn in range(2):
        for shift in range(2):
            piece = by_shift[shift]
            if turn or shift:
                pairs = [(i, i ^ shift ^ (96 * turn)) for i in range(DEVICES)]
                piece = lax.ppermute(piece, EVERY, pairs)
            q_pieces.append(piece)

    own, q_pieces[1:] = lax.optimization_barrier((own, q_pieces[1:]))
    other = lax.ppermute(own, EVERY, [(i, i ^ 1) for i in range(DEVICES)])
    partial = attend(place, q_pieces, own, other)
    got = lax.all_to_all(partial, EVERY, 0, 0, axis_index_groups=OUTPUT_GROUPS)
    mixed, logs = merge(got)
    return (mixed, logs.T)


def solution(mesh):
    placed = (P("qrow", "kcol"), P(("kcol", "qrow"), None), P(("kcol", "qrow"), None))
    return jax.shard_map(
        per_device,
        mesh=mesh,
        in_specs=placed,
        out_specs=(P(("qrow", "kcol"), None), P(("qrow", "kcol"), None)),
        check_vma=False,
    )
```

```python
import functools
import math

import jax
import jax.numpy as jnp
from jax import lax
from jax.experimental import pallas as pl
from jax.experimental.pallas import tpu as pltpu
from jax.sharding import PartitionSpec as P

HQ = 32
KVH = 4
HD = 128
GROUP = 8
EVERY = ("qrow", "kcol")
SPANS = 8
DEVICES = 128
SIDES = 4

NEG_FILL = -1e30
LOG2E = math.log2(math.e)
LN2 = math.log(2.0)
HELD = 4
DEPTH = 136


def device_at(span, side, slot):
    return span * 16 + side * 4 + slot


KEY_GROUPS = [
    [
        device_at(half * 4 + near, side, xh * 2 + core)
        for near in range(4)
        for xh in range(2)
        for side in range(SIDES)
    ]
    for half in range(2)
    for core in range(2)
]
OUTPUT_GROUPS = [
    [
        device_at(span, side, xh * 2 + core)
        for span in (low, low ^ 6)
        for side in range(SIDES)
        for xh in range(2)
    ]
    for low in range(SPANS // 2)
    for core in range(2)
]


def swapped(array, bits):
    return lax.ppermute(array, EVERY, [(i, i ^ bits) for i in range(DEVICES)])


def pack_body(key_ref, value_ref, out_ref):
    for side in range(SIDES):
        cols = slice(side * HD, (side + 1) * HD)
        for copy in range(8):
            out_ref[copy * SIDES + side, :, :HD] = key_ref[:, cols]
            out_ref[copy * SIDES + side, :, HD:] = value_ref[:, cols]


def pack(key_states, value_states):
    whole = pl.BlockSpec(memory_space=pltpu.VMEM)
    return pl.pallas_call(
        pack_body,
        out_shape=jax.ShapeDtypeStruct((32, 64, 2 * HD), jnp.bfloat16),
        in_specs=[whole, whole],
        out_specs=whole,
        name="pack",
    )(key_states, value_states)


def split_body(place, own_ref, couple_ref, kept_ref, given_ref):
    core = place[1] & 1
    for shift, out_ref in ((0, kept_ref), (1, given_ref)):
        for turn, ref in enumerate((own_ref, couple_ref)):
            for piece in range(8):
                at = pl.multiple_of(piece * 128 + (core ^ shift) * 64, 64)
                out_ref[turn, piece] = ref[pl.ds(at, 64), :]


def split(place, own, couple):
    whole = pl.BlockSpec(memory_space=pltpu.VMEM)
    return pl.pallas_call(
        split_body,
        out_shape=[jax.ShapeDtypeStruct((2, 8, 64, 2 * HD), jnp.bfloat16)] * 2,
        in_specs=[pl.BlockSpec(memory_space=pltpu.SMEM), whole, whole],
        out_specs=[whole] * 2,
        cost_estimate=pl.CostEstimate(
            flops=2 * 10**10, bytes_accessed=2**21, transcendentals=0
        ),
        compiler_params=pltpu.CompilerParams(vmem_limit_bytes=8 * 2**20),
        name="split",
    )(place, own, couple)


def grouped(scores):
    return scores.reshape(scores.shape[0] // 8, 8, scores.shape[1])


def highest(parts):
    high = functools.reduce(jnp.maximum, [jnp.max(grouped(part), axis=0) for part in parts])
    return jnp.broadcast_to(jnp.max(high, axis=0, keepdims=True), high.shape)


def exponentials(parts, peak):
    return [
        jnp.exp2(grouped(part) - peak[None]).reshape(part.shape) for part in parts
    ]


def summed(parts):
    return functools.reduce(jnp.add, [jnp.sum(grouped(part), axis=0) for part in parts])


def attend_body(place, *refs):
    q_refs = refs[:2]
    own_ref, other_ref, o_ref, q_all, keys, values, acc, top, total, key_size, safe_now = refs[2:]
    row, column = place[0], place[1]
    half, core = row >> 2, column & 1

    for ref, part in ((own_ref, core), (other_ref, 1 - core)):
        for block in range(8):
            side, xh = block // 2, block % 2
            for near in range(4):
                held = pl.ds(pl.multiple_of(part * 256 + near * 64, 64), 64)
                piece = (near * 2 + xh) * SIDES + side
                keys[block, held, :] = ref[piece, :, :HD]
                values[block, held, :] = ref[piece, :, HD:]

    def lengths(vectors):
        return lax.dot_general(
            jnp.ones((8, HD), jnp.bfloat16),
            vectors * vectors,
            (((1,), (1,)), ((), ())),
            preferred_element_type=jnp.float32,
        )

    for block in range(7):
        key_size[block] = lengths(keys[block])

    def score(tile, block, width):
        return lax.dot_general(
            keys[block, :width, :],
            q_all[tile * 512 : (tile + 1) * 512, :],
            (((1,), (1,)), ((), ())),
            preferred_element_type=jnp.float32,
        ) * (LOG2E / math.sqrt(HD))

    def gathered(blocks, weights):
        return sum(
            lax.dot_general(
                values[block, : weight.shape[0], :],
                weight.astype(jnp.bfloat16),
                (((0,), (0,)), ((), ())),
                preferred_element_type=jnp.float32,
            )
            for block, weight in zip(blocks, weights)
        )

    def weigh(tile, parts):
        old = top[tile]
        new = jnp.maximum(old, highest(parts))
        scale = jnp.exp2(old - new)
        weights = exponentials(parts, new)
        top[tile] = new
        total[tile] = total[tile] * scale + summed(weights)
        return weights, scale

    def add(tile, blocks, weights, scale):
        acc[tile] = acc[tile] * scale[:1] + gathered(blocks, weights)

    in_key = lax.broadcasted_iota(jnp.int32, (256, 512), 0)
    in_tile = lax.broadcasted_iota(jnp.int32, (256, 512), 1)
    in_row = (in_tile >> 8) * 128 + (in_tile & 63)
    for turn in range(2):
        span = row if turn == 0 else row ^ 6
        member = (row >> 2) ^ turn
        for shift in range(2):
            for piece in range(8):
                for head in range(2):
                    at = piece * 256 + (core ^ shift) * 128 + head * 64
                    q_all[pl.ds(pl.multiple_of(at, 64), 64), :] = q_refs[shift][
                        turn, piece, :, head * HD : (head + 1) * HD
                    ]

        def ahead(tile):
            return score(tile, span, 256 if tile < 2 else 512)

        ready = ahead(0)
        for tile in range(4):
            later = ahead(tile + 1) if tile < 3 else None
            edge, parts = ready[-256:], [ready[:256]] if tile >= 2 else []
            reach = in_row + (tile % 2) * 256 + core * 64 - half * 256
            keep = in_key <= reach
            edge = jnp.where(keep, edge, NEG_FILL)
            peak = highest(parts + [edge])
            weights = exponentials(parts, peak)
            weights.append(jnp.where(keep, exponentials([edge], peak)[0], 0.0))
            top[tile] = peak
            total[tile] = summed(weights)
            acc[tile] = gathered([span], [jnp.concatenate(weights, axis=0)])
            ready = later

        longest = jnp.zeros((8, 512), jnp.float32)
        for block in range(7):
            longest = jnp.maximum(longest, jnp.where(block < span, key_size[block], 0.0))
        longest = jnp.max(longest)

        def settle():
            fixed, width, lift = [], [], []
            for tile in range(4):
                squares = lengths(q_all[tile * 512 : (tile + 1) * 512, :])
                bound = jnp.sqrt(squares * longest) * (1.004 * LOG2E / math.sqrt(HD))
                some = top[tile] > 0.5 * NEG_FILL
                low = jnp.where(some, top[tile], -bound)
                fixed.append(jnp.maximum(low, bound - 112.0))
                width.append(bound - low)
                lift.append(jnp.where(some, fixed[tile] - low, 0.0))
            calm = jnp.max(functools.reduce(jnp.maximum, width)) <= 212.0
            lifted = jnp.max(functools.reduce(jnp.maximum, lift)) > 0.0
            safe_now[0] = calm.astype(jnp.int32)

            @pl.when(jnp.logical_and(calm, lifted))
            def _():
                for tile in range(4):
                    scale = jnp.exp2(top[tile] - fixed[tile])
                    total[tile] = total[tile] * scale
                    acc[tile] = acc[tile] * scale[:1]

            @pl.when(calm)
            def _():
                for tile in range(4):
                    top[tile] = fixed[tile]

        settle()

        def sweep(blocks):
            units = [(tile, block, at) for block in blocks for tile in range(4) for at in range(0, 512, 512)]

            def unit_score(unit):
                tile, block, at = unit
                return lax.dot_general(
                    keys[block, at : at + 512, :],
                    q_all[tile * 512 : (tile + 1) * 512, :],
                    (((1,), (1,)), ((), ())),
                    preferred_element_type=jnp.float32,
                ) * (LOG2E / math.sqrt(HD))

            def unit_add(unit, weight):
                tile, block, at = unit
                acc[tile] += lax.dot_general(
                    values[block, at : at + 512, :],
                    weight,
                    (((0,), (0,)), ((), ())),
                    preferred_element_type=jnp.float32,
                )

            ready, waiting = unit_score(units[0]), None
            for index, unit in enumerate(units):
                later = unit_score(units[index + 1]) if index + 1 < len(units) else None
                weight = exponentials([ready], top[unit[0]])[0]
                total[unit[0]] += summed([weight])
                if waiting is not None:
                    unit_add(units[index - 1], waiting)
                waiting, ready = weight.astype(jnp.bfloat16), later
            unit_add(units[-1], waiting)

        def exact_sweep(block):
            for tile in range(4):
                weights, scale = weigh(tile, [score(tile, block, 512)])
                add(tile, [block], weights, scale)

        @pl.loop(0, span // 2)
        def _(group):
            calm = safe_now[0]

            @pl.when(calm == 1)
            def _():
                sweep([group * 2 + i for i in range(2)])

            @pl.when(calm == 0)
            def _():
                for i in range(2):
                    exact_sweep(group * 2 + i)
                settle()

        @pl.when((span & 1) == 1)
        def _():
            calm = safe_now[0]

            @pl.when(calm == 1)
            def _():
                sweep([span - 1])

            @pl.when(calm == 0)
            def _():
                exact_sweep(span - 1)

        term = lax.broadcasted_iota(jnp.int32, (8, 512), 0)
        for tile in range(4):
            whole = jnp.sum(total[tile], axis=0, keepdims=True)
            some = whole > 0
            safe = jnp.where(some, whole, 1.0)
            normed = (acc[tile] * (1.0 / safe)).astype(jnp.bfloat16)
            stat = jnp.where(some, (top[tile] + jnp.log2(safe)) * LN2, NEG_FILL)
            coarse = stat.astype(jnp.bfloat16).astype(jnp.float32)
            middle = (stat - coarse).astype(jnp.bfloat16).astype(jnp.float32)
            fine = stat - coarse - middle
            terms = jnp.where(term == 0, coarse, jnp.where(term == 1, middle, fine))
            for part in range(2):
                cols = slice(part * 256, (part + 1) * 256)
                at = member * 8 + tile * 2 + part
                o_ref[at, :HD, :] = normed[:, cols]
                o_ref[at, HD:, :] = terms[:, cols].astype(jnp.bfloat16)


def attend(place, q_pieces, own, other):
    whole = pl.BlockSpec(memory_space=pltpu.VMEM)
    return pl.pallas_call(
        attend_body,
        out_shape=jax.ShapeDtypeStruct((16, DEPTH, 256), jnp.bfloat16),
        in_specs=[pl.BlockSpec(memory_space=pltpu.SMEM)] + [whole] * 4,
        out_specs=whole,
        scratch_shapes=[
            pltpu.VMEM((2048, HD), jnp.bfloat16),
            pltpu.VMEM((8, 512, HD), jnp.bfloat16),
            pltpu.VMEM((8, 512, HD), jnp.bfloat16),
            pltpu.VMEM((4, HD, 512), jnp.float32),
            pltpu.VMEM((4, 8, 512), jnp.float32),
            pltpu.VMEM((4, 8, 512), jnp.float32),
            pltpu.VMEM((7, 8, 512), jnp.float32),
            pltpu.SMEM((1,), jnp.int32),
        ],
        compiler_params=pltpu.CompilerParams(vmem_limit_bytes=32 * 2**20),
        cost_estimate=pl.CostEstimate(
            flops=36 * 4 * 512 * 512 * HD,
            bytes_accessed=4 * 2**20,
            transcendentals=36 * 512 * 512,
        ),
        name="attend",
    )(place, *q_pieces, own, other)


def merge_body(got_ref, mixed_ref, log_ref):
    for block in range(2 * SIDES):
        sums = []
        for member in range(2):
            terms = got_ref[member, block, HD:, :].astype(jnp.float32)
            sums.append(terms[0:1] + terms[1:2] + terms[2:3])
        high = jnp.maximum(sums[0], sums[1])
        joint = high + jnp.log(jnp.exp(sums[0] - high) + jnp.exp(sums[1] - high))
        mixed = got_ref[0, block, :HD, :].astype(jnp.float32) * jnp.exp(sums[0] - joint) + (
            got_ref[1, block, :HD, :].astype(jnp.float32) * jnp.exp(sums[1] - joint)
        )
        for pair in range(2):
            rows = mixed[:, pair * HD : (pair + 1) * HD].T.astype(jnp.bfloat16)
            for head in range(2):
                place = block * HELD + pair * 2 + head
                mixed_ref[:, place * HD : (place + 1) * HD] = rows[head * 64 : (head + 1) * 64]
                at = (pair * 2 + head) * 64
                log_ref[place : place + 1, :] = joint[:, at : at + 64]


def merge(got):
    whole = pl.BlockSpec(memory_space=pltpu.VMEM)
    return pl.pallas_call(
        merge_body,
        out_shape=(
            jax.ShapeDtypeStruct((64, HQ * HD), jnp.bfloat16),
            jax.ShapeDtypeStruct((HQ, 64), jnp.float32),
        ),
        in_specs=[whole],
        out_specs=(whole, whole),
        compiler_params=pltpu.CompilerParams(vmem_limit_bytes=8 * 2**20),
        name="merge",
    )(got.reshape(2, 2 * SIDES, DEPTH, 256))


def per_device(queries, key_states, value_states):
    row = lax.axis_index("qrow")
    column = lax.axis_index("kcol")
    place = jnp.stack([row, column])

    couple = swapped(queries, 96)
    own = lax.all_to_all(
        pack(key_states, value_states), EVERY, 0, 0, axis_index_groups=KEY_GROUPS
    )

    kept, given = split(place, queries, couple)
    taken = swapped(given, 1)

    own, taken = lax.optimization_barrier((own, taken))
    q_pieces = [kept, taken]
    other = swapped(own, 1)
    partial = attend(place, q_pieces, own, other)
    got = lax.all_to_all(partial, EVERY, 0, 0, axis_index_groups=OUTPUT_GROUPS)
    mixed, logs = merge(got)
    return (mixed, logs.T)


def solution(mesh):
    placed = (P("qrow", "kcol"), P(("kcol", "qrow"), None), P(("kcol", "qrow"), None))
    return jax.shard_map(
        per_device,
        mesh=mesh,
        in_specs=placed,
        out_specs=(P(("qrow", "kcol"), None), P(("qrow", "kcol"), None)),
        check_vma=False,
    )
```

```python
import functools
import math

import jax
import jax.numpy as jnp
from jax import lax
from jax.experimental import pallas as pl
from jax.experimental.pallas import tpu as pltpu
from jax.sharding import PartitionSpec as P

HQ = 32
KVH = 4
HD = 128
GROUP = 8
EVERY = ("qrow", "kcol")
SPANS = 8
DEVICES = 128
SIDES = 4

NEG_FILL = -1e30
LOG2E = math.log2(math.e)
LN2 = math.log(2.0)
HELD = 4
DEPTH = 136


def device_at(span, side, slot):
    return span * 16 + side * 4 + slot


KEY_GROUPS = [
    [
        device_at(half * 4 + near, side, xh * 2 + core)
        for near in range(4)
        for xh in range(2)
        for side in range(SIDES)
    ]
    for half in range(2)
    for core in range(2)
]
OUTPUT_GROUPS = [
    [
        device_at(span, side, xh * 2 + core)
        for span in (low, low ^ 6)
        for side in range(SIDES)
        for xh in range(2)
    ]
    for low in range(SPANS // 2)
    for core in range(2)
]


def swapped(array, bits):
    return lax.ppermute(array, EVERY, [(i, i ^ bits) for i in range(DEVICES)])


def pack_body(key_ref, value_ref, out_ref):
    for side in range(SIDES):
        cols = slice(side * HD, (side + 1) * HD)
        for copy in range(8):
            out_ref[copy * SIDES + side, :, :HD] = key_ref[:, cols]
            out_ref[copy * SIDES + side, :, HD:] = value_ref[:, cols]


def pack(key_states, value_states):
    whole = pl.BlockSpec(memory_space=pltpu.VMEM)
    return pl.pallas_call(
        pack_body,
        out_shape=jax.ShapeDtypeStruct((32, 64, 2 * HD), jnp.bfloat16),
        in_specs=[whole, whole],
        out_specs=whole,
        name="pack",
    )(key_states, value_states)


def split_body(place, own_ref, couple_ref, kept_ref, given_ref):
    core = place[1] & 1
    for shift, out_ref in ((0, kept_ref), (1, given_ref)):
        for turn, ref in enumerate((own_ref, couple_ref)):
            for piece in range(8):
                at = pl.multiple_of(piece * 128 + (core ^ shift) * 64, 64)
                out_ref[turn, piece] = ref[pl.ds(at, 64), :]


def split(place, own, couple):
    whole = pl.BlockSpec(memory_space=pltpu.VMEM)
    return pl.pallas_call(
        split_body,
        out_shape=[jax.ShapeDtypeStruct((2, 8, 64, 2 * HD), jnp.bfloat16)] * 2,
        in_specs=[pl.BlockSpec(memory_space=pltpu.SMEM), whole, whole],
        out_specs=[whole] * 2,
        cost_estimate=pl.CostEstimate(
            flops=2 * 10**10, bytes_accessed=2**21, transcendentals=0
        ),
        compiler_params=pltpu.CompilerParams(vmem_limit_bytes=8 * 2**20),
        name="split",
    )(place, own, couple)


def grouped(scores):
    return scores.reshape(scores.shape[0] // 8, 8, scores.shape[1])


def highest(parts):
    high = functools.reduce(jnp.maximum, [jnp.max(grouped(part), axis=0) for part in parts])
    return jnp.broadcast_to(jnp.max(high, axis=0, keepdims=True), high.shape)


def exponentials(parts, peak):
    return [
        jnp.exp2(grouped(part) - peak[None]).reshape(part.shape) for part in parts
    ]


def summed(parts):
    return functools.reduce(jnp.add, [jnp.sum(grouped(part), axis=0) for part in parts])


def lengths(vectors):
    return lax.dot_general(
        jnp.ones((8, HD), jnp.bfloat16),
        vectors * vectors,
        (((1,), (1,)), ((), ())),
        preferred_element_type=jnp.float32,
    )


def arrange_body(place, kept_ref, taken_ref, q_both, q_size):
    core = place[1] & 1
    for turn in range(2):
        for shift, ref in ((0, kept_ref), (1, taken_ref)):
            for piece in range(8):
                for head in range(2):
                    at = piece * 256 + (core ^ shift) * 128 + head * 64
                    q_both[turn, pl.ds(pl.multiple_of(at, 64), 64), :] = ref[
                        turn, piece, :, head * HD : (head + 1) * HD
                    ]
        for tile in range(4):
            q_size[turn, tile] = lengths(q_both[turn, tile * 512 : (tile + 1) * 512, :])


def arrange(place, kept, taken):
    whole = pl.BlockSpec(memory_space=pltpu.VMEM)
    return pl.pallas_call(
        arrange_body,
        out_shape=[
            jax.ShapeDtypeStruct((2, 2048, HD), jnp.bfloat16),
            jax.ShapeDtypeStruct((2, 4, 8, 512), jnp.float32),
        ],
        in_specs=[pl.BlockSpec(memory_space=pltpu.SMEM), whole, whole],
        out_specs=[whole, whole],
        compiler_params=pltpu.CompilerParams(vmem_limit_bytes=8 * 2**20),
        name="arrange",
    )(place, kept, taken)


def attend_body(place, *refs):
    q_both, q_size, own_ref, other_ref, o_ref = refs[:5]
    keys, values, acc, top, total, key_size, safe_now = refs[5:]
    row, column = place[0], place[1]
    half, core = row >> 2, column & 1

    for ref, part in ((own_ref, core), (other_ref, 1 - core)):
        for block in range(8):
            side, xh = block // 2, block % 2
            for near in range(4):
                held = pl.ds(pl.multiple_of(part * 256 + near * 64, 64), 64)
                piece = (near * 2 + xh) * SIDES + side
                keys[block, held, :] = ref[piece, :, :HD]
                values[block, held, :] = ref[piece, :, HD:]

    for block in range(7):
        key_size[block] = lengths(keys[block])

    def score(q_all, tile, block, width):
        return lax.dot_general(
            keys[block, :width, :],
            q_all[tile * 512 : (tile + 1) * 512, :],
            (((1,), (1,)), ((), ())),
            preferred_element_type=jnp.float32,
        ) * (LOG2E / math.sqrt(HD))

    def gathered(blocks, weights):
        return sum(
            lax.dot_general(
                values[block, : weight.shape[0], :],
                weight.astype(jnp.bfloat16),
                (((0,), (0,)), ((), ())),
                preferred_element_type=jnp.float32,
            )
            for block, weight in zip(blocks, weights)
        )

    def weigh(tile, parts):
        old = top[tile]
        new = jnp.maximum(old, highest(parts))
        scale = jnp.exp2(old - new)
        weights = exponentials(parts, new)
        top[tile] = new
        total[tile] = total[tile] * scale + summed(weights)
        return weights, scale

    def add(tile, blocks, weights, scale):
        acc[tile] = acc[tile] * scale[:1] + gathered(blocks, weights)

    in_key = lax.broadcasted_iota(jnp.int32, (256, 512), 0)
    in_tile = lax.broadcasted_iota(jnp.int32, (256, 512), 1)
    in_row = (in_tile >> 8) * 128 + (in_tile & 63)
    for turn in range(2):
        span = row if turn == 0 else row ^ 6
        member = (row >> 2) ^ turn
        q_all = q_both.at[turn]

        def ahead(tile):
            return score(q_all, tile, span, 256 if tile < 2 else 512)

        ready = ahead(0)
        for tile in range(4):
            later = ahead(tile + 1) if tile < 3 else None
            edge, parts = ready[-256:], [ready[:256]] if tile >= 2 else []
            reach = in_row + (tile % 2) * 256 + core * 64 - half * 256
            keep = in_key <= reach
            edge = jnp.where(keep, edge, NEG_FILL)
            peak = highest(parts + [edge])
            weights = exponentials(parts, peak)
            weights.append(jnp.where(keep, exponentials([edge], peak)[0], 0.0))
            top[tile] = peak
            total[tile] = summed(weights)
            acc[tile] = gathered([span], [jnp.concatenate(weights, axis=0)])
            ready = later

        longest = jnp.zeros((8, 512), jnp.float32)
        for block in range(7):
            longest = jnp.maximum(longest, jnp.where(block < span, key_size[block], 0.0))
        longest = jnp.max(longest)

        def settle():
            fixed, width, lift = [], [], []
            for tile in range(4):
                bound = jnp.sqrt(q_size[turn, tile] * longest) * (1.004 * LOG2E / math.sqrt(HD))
                some = top[tile] > 0.5 * NEG_FILL
                low = jnp.where(some, top[tile], -bound)
                fixed.append(jnp.maximum(low, bound - 112.0))
                width.append(bound - low)
                lift.append(jnp.where(some, fixed[tile] - low, 0.0))
            calm = jnp.max(functools.reduce(jnp.maximum, width)) <= 212.0
            lifted = jnp.max(functools.reduce(jnp.maximum, lift)) > 0.0
            safe_now[0] = calm.astype(jnp.int32)

            @pl.when(jnp.logical_and(calm, lifted))
            def _():
                for tile in range(4):
                    scale = jnp.exp2(top[tile] - fixed[tile])
                    total[tile] = total[tile] * scale
                    acc[tile] = acc[tile] * scale[:1]

            @pl.when(calm)
            def _():
                for tile in range(4):
                    top[tile] = fixed[tile]

        settle()

        def sweep(blocks):
            units = [(tile, block, at) for block in blocks for tile in range(4) for at in range(0, 512, 512)]

            def unit_score(unit):
                tile, block, at = unit
                return lax.dot_general(
                    keys[block, at : at + 512, :],
                    q_all[tile * 512 : (tile + 1) * 512, :],
                    (((1,), (1,)), ((), ())),
                    preferred_element_type=jnp.float32,
                ) * (LOG2E / math.sqrt(HD))

            def unit_add(unit, weight):
                tile, block, at = unit
                acc[tile] += lax.dot_general(
                    values[block, at : at + 512, :],
                    weight,
                    (((0,), (0,)), ((), ())),
                    preferred_element_type=jnp.float32,
                )

            ready, waiting = unit_score(units[0]), None
            for index, unit in enumerate(units):
                later = unit_score(units[index + 1]) if index + 1 < len(units) else None
                weight = exponentials([ready], top[unit[0]])[0]
                total[unit[0]] += summed([weight])
                if waiting is not None:
                    unit_add(units[index - 1], waiting)
                waiting, ready = weight.astype(jnp.bfloat16), later
            unit_add(units[-1], waiting)

        def exact_sweep(block):
            for tile in range(4):
                weights, scale = weigh(tile, [score(q_all, tile, block, 512)])
                add(tile, [block], weights, scale)

        @pl.loop(0, span // 2)
        def _(group):
            calm = safe_now[0]

            @pl.when(calm == 1)
            def _():
                sweep([group * 2 + i for i in range(2)])

            @pl.when(calm == 0)
            def _():
                for i in range(2):
                    exact_sweep(group * 2 + i)
                settle()

        @pl.when((span & 1) == 1)
        def _():
            calm = safe_now[0]

            @pl.when(calm == 1)
            def _():
                sweep([span - 1])

            @pl.when(calm == 0)
            def _():
                exact_sweep(span - 1)

        term = lax.broadcasted_iota(jnp.int32, (8, 512), 0)
        for tile in range(4):
            whole = jnp.sum(total[tile], axis=0, keepdims=True)
            some = whole > 0
            safe = jnp.where(some, whole, 1.0)
            normed = (acc[tile] * (1.0 / safe)).astype(jnp.bfloat16)
            stat = jnp.where(some, (top[tile] + jnp.log2(safe)) * LN2, NEG_FILL)
            coarse = stat.astype(jnp.bfloat16).astype(jnp.float32)
            middle = (stat - coarse).astype(jnp.bfloat16).astype(jnp.float32)
            fine = stat - coarse - middle
            terms = jnp.where(term == 0, coarse, jnp.where(term == 1, middle, fine))
            for part in range(2):
                cols = slice(part * 256, (part + 1) * 256)
                at = member * 8 + tile * 2 + part
                o_ref[at, :HD, :] = normed[:, cols]
                o_ref[at, HD:, :] = terms[:, cols].astype(jnp.bfloat16)


def attend(place, q_pieces, own, other):
    whole = pl.BlockSpec(memory_space=pltpu.VMEM)
    return pl.pallas_call(
        attend_body,
        out_shape=jax.ShapeDtypeStruct((16, DEPTH, 256), jnp.bfloat16),
        in_specs=[pl.BlockSpec(memory_space=pltpu.SMEM)] + [whole] * 4,
        out_specs=whole,
        scratch_shapes=[
            pltpu.VMEM((8, 512, HD), jnp.bfloat16),
            pltpu.VMEM((8, 512, HD), jnp.bfloat16),
            pltpu.VMEM((4, HD, 512), jnp.float32),
            pltpu.VMEM((4, 8, 512), jnp.float32),
            pltpu.VMEM((4, 8, 512), jnp.float32),
            pltpu.VMEM((7, 8, 512), jnp.float32),
            pltpu.SMEM((1,), jnp.int32),
        ],
        compiler_params=pltpu.CompilerParams(vmem_limit_bytes=32 * 2**20),
        cost_estimate=pl.CostEstimate(
            flops=36 * 4 * 512 * 512 * HD,
            bytes_accessed=4 * 2**20,
            transcendentals=36 * 512 * 512,
        ),
        name="attend",
    )(place, *q_pieces, own, other)


def merge_body(got_ref, mixed_ref, log_ref):
    for block in range(2 * SIDES):
        sums = []
        for member in range(2):
            terms = got_ref[member, block, HD:, :].astype(jnp.float32)
            sums.append(terms[0:1] + terms[1:2] + terms[2:3])
        high = jnp.maximum(sums[0], sums[1])
        joint = high + jnp.log(jnp.exp(sums[0] - high) + jnp.exp(sums[1] - high))
        mixed = got_ref[0, block, :HD, :].astype(jnp.float32) * jnp.exp(sums[0] - joint) + (
            got_ref[1, block, :HD, :].astype(jnp.float32) * jnp.exp(sums[1] - joint)
        )
        for pair in range(2):
            rows = mixed[:, pair * HD : (pair + 1) * HD].T.astype(jnp.bfloat16)
            for head in range(2):
                place = block * HELD + pair * 2 + head
                mixed_ref[:, place * HD : (place + 1) * HD] = rows[head * 64 : (head + 1) * 64]
                at = (pair * 2 + head) * 64
                log_ref[place : place + 1, :] = joint[:, at : at + 64]


def merge(got):
    whole = pl.BlockSpec(memory_space=pltpu.VMEM)
    return pl.pallas_call(
        merge_body,
        out_shape=(
            jax.ShapeDtypeStruct((64, HQ * HD), jnp.bfloat16),
            jax.ShapeDtypeStruct((HQ, 64), jnp.float32),
        ),
        in_specs=[whole],
        out_specs=(whole, whole),
        compiler_params=pltpu.CompilerParams(vmem_limit_bytes=8 * 2**20),
        name="merge",
    )(got.reshape(2, 2 * SIDES, DEPTH, 256))


def per_device(queries, key_states, value_states):
    row = lax.axis_index("qrow")
    column = lax.axis_index("kcol")
    place = jnp.stack([row, column])

    couple = swapped(queries, 96)
    own = lax.all_to_all(
        pack(key_states, value_states), EVERY, 0, 0, axis_index_groups=KEY_GROUPS
    )

    kept, given = split(place, queries, couple)
    taken = swapped(given, 1)

    arranged = arrange(place, kept, taken)
    own, arranged = lax.optimization_barrier((own, arranged))
    other = swapped(own, 1)
    partial = attend(place, arranged, own, other)
    got = lax.all_to_all(partial, EVERY, 0, 0, axis_index_groups=OUTPUT_GROUPS)
    mixed, logs = merge(got)
    return (mixed, logs.T)


def solution(mesh):
    placed = (P("qrow", "kcol"), P(("kcol", "qrow"), None), P(("kcol", "qrow"), None))
    return jax.shard_map(
        per_device,
        mesh=mesh,
        in_specs=placed,
        out_specs=(P(("qrow", "kcol"), None), P(("qrow", "kcol"), None)),
        check_vma=False,
    )
```

```python
import functools
import math

import jax
import jax.numpy as jnp
from jax import lax
from jax.experimental import pallas as pl
from jax.experimental.pallas import tpu as pltpu
from jax.sharding import PartitionSpec as P

HQ = 32
KVH = 4
HD = 128
GROUP = 8
EVERY = ("qrow", "kcol")
SPANS = 8
DEVICES = 128
SIDES = 4

NEG_FILL = -1e30
LOG2E = math.log2(math.e)
LN2 = math.log(2.0)
HELD = 4
DEPTH = 136


def device_at(span, side, slot):
    return span * 16 + side * 4 + slot


KEY_GROUPS = [
    [
        device_at(half * 4 + near, side, xh * 2 + core)
        for near in range(4)
        for xh in range(2)
        for side in range(SIDES)
    ]
    for half in range(2)
    for core in range(2)
]
OUTPUT_GROUPS = [
    [
        device_at(span, side, xh * 2 + core)
        for span in (low, low ^ 6)
        for side in range(SIDES)
        for xh in range(2)
    ]
    for low in range(SPANS // 2)
    for core in range(2)
]


def swapped(array, bits):
    return lax.ppermute(array, EVERY, [(i, i ^ bits) for i in range(DEVICES)])


def pack_body(key_ref, value_ref, out_ref):
    for side in range(SIDES):
        cols = slice(side * HD, (side + 1) * HD)
        for copy in range(8):
            out_ref[copy * SIDES + side, :, :HD] = key_ref[:, cols]
            out_ref[copy * SIDES + side, :, HD:] = value_ref[:, cols]


def pack(key_states, value_states):
    whole = pl.BlockSpec(memory_space=pltpu.VMEM)
    return pl.pallas_call(
        pack_body,
        out_shape=jax.ShapeDtypeStruct((32, 64, 2 * HD), jnp.bfloat16),
        in_specs=[whole, whole],
        out_specs=whole,
        name="pack",
    )(key_states, value_states)


def split_body(place, own_ref, couple_ref, kept_ref, given_ref):
    core = place[1] & 1
    for shift, out_ref in ((0, kept_ref), (1, given_ref)):
        for turn, ref in enumerate((own_ref, couple_ref)):
            for piece in range(8):
                at = pl.multiple_of(piece * 128 + (core ^ shift) * 64, 64)
                out_ref[turn, piece] = ref[pl.ds(at, 64), :]


def split(place, own, couple):
    whole = pl.BlockSpec(memory_space=pltpu.VMEM)
    return pl.pallas_call(
        split_body,
        out_shape=[jax.ShapeDtypeStruct((2, 8, 64, 2 * HD), jnp.bfloat16)] * 2,
        in_specs=[pl.BlockSpec(memory_space=pltpu.SMEM), whole, whole],
        out_specs=[whole] * 2,
        cost_estimate=pl.CostEstimate(
            flops=2 * 10**10, bytes_accessed=2**21, transcendentals=0
        ),
        compiler_params=pltpu.CompilerParams(vmem_limit_bytes=8 * 2**20),
        name="split",
    )(place, own, couple)


def grouped(scores):
    return scores.reshape(scores.shape[0] // 8, 8, scores.shape[1])


def highest(parts):
    high = functools.reduce(jnp.maximum, [jnp.max(grouped(part), axis=0) for part in parts])
    return jnp.broadcast_to(jnp.max(high, axis=0, keepdims=True), high.shape)


def exponentials(parts, peak):
    return [
        jnp.exp2(grouped(part) - peak[None]).reshape(part.shape) for part in parts
    ]


def summed(parts):
    return functools.reduce(jnp.add, [jnp.sum(grouped(part), axis=0) for part in parts])


def lengths(vectors):
    return lax.dot_general(
        jnp.ones((8, HD), jnp.bfloat16),
        vectors * vectors,
        (((1,), (1,)), ((), ())),
        preferred_element_type=jnp.float32,
    )


def arrange_body(place, kept_ref, taken_ref, q_both, q_size):
    core = place[1] & 1
    for turn in range(2):
        for shift, ref in ((0, kept_ref), (1, taken_ref)):
            for piece in range(8):
                for head in range(2):
                    at = piece * 256 + (core ^ shift) * 128 + head * 64
                    q_both[turn, pl.ds(pl.multiple_of(at, 64), 64), :] = ref[
                        turn, piece, :, head * HD : (head + 1) * HD
                    ]
        for tile in range(4):
            q_size[turn, tile] = lengths(q_both[turn, tile * 512 : (tile + 1) * 512, :])


def arrange(place, kept, taken):
    whole = pl.BlockSpec(memory_space=pltpu.VMEM)
    return pl.pallas_call(
        arrange_body,
        out_shape=[
            jax.ShapeDtypeStruct((2, 2048, HD), jnp.bfloat16),
            jax.ShapeDtypeStruct((2, 4, 8, 512), jnp.float32),
        ],
        in_specs=[pl.BlockSpec(memory_space=pltpu.SMEM), whole, whole],
        out_specs=[whole, whole],
        compiler_params=pltpu.CompilerParams(vmem_limit_bytes=8 * 2**20),
        name="arrange",
    )(place, kept, taken)


def attend_body(place, *refs):
    q_both, q_size, own_ref, other_ref, o_ref = refs[:5]
    keys, values, acc, top, total, key_size, safe_now = refs[5:]
    row, column = place[0], place[1]
    half, core = row >> 2, column & 1

    for ref, part in ((own_ref, core), (other_ref, 1 - core)):
        for block in range(8):
            side, xh = block // 2, block % 2
            for near in range(4):
                held = pl.ds(pl.multiple_of(part * 256 + near * 64, 64), 64)
                piece = (near * 2 + xh) * SIDES + side
                keys[block, held, :] = ref[piece, :, :HD]
                values[block, held, :] = ref[piece, :, HD:]

    for block in range(7):
        key_size[block] = lengths(keys[block])

    def score(q_all, tile, block, width):
        return lax.dot_general(
            keys[block, :width, :],
            q_all[tile * 512 : (tile + 1) * 512, :],
            (((1,), (1,)), ((), ())),
            preferred_element_type=jnp.float32,
        ) * (LOG2E / math.sqrt(HD))

    def gathered(blocks, weights):
        return sum(
            lax.dot_general(
                values[block, : weight.shape[0], :],
                weight.astype(jnp.bfloat16),
                (((0,), (0,)), ((), ())),
                preferred_element_type=jnp.float32,
            )
            for block, weight in zip(blocks, weights)
        )

    def weigh(tile, parts):
        old = top[tile]
        new = jnp.maximum(old, highest(parts))
        scale = jnp.exp2(old - new)
        weights = exponentials(parts, new)
        top[tile] = new
        total[tile] = total[tile] * scale + summed(weights)
        return weights, scale

    def add(tile, blocks, weights, scale):
        acc[tile] = acc[tile] * scale[:1] + gathered(blocks, weights)

    in_key = lax.broadcasted_iota(jnp.int32, (256, 512), 0)
    in_tile = lax.broadcasted_iota(jnp.int32, (256, 512), 1)
    in_row = (in_tile >> 8) * 128 + (in_tile & 63)
    for turn in range(2):
        span = row if turn == 0 else row ^ 6
        member = (row >> 2) ^ turn
        q_all = q_both.at[turn]

        def ahead(tile):
            return score(q_all, tile, span, 256 if tile < 2 else 512)

        ready = ahead(0)
        for tile in range(4):
            later = ahead(tile + 1) if tile < 3 else None
            edge, parts = ready[-256:], [ready[:256]] if tile >= 2 else []
            reach = in_row + (tile % 2) * 256 + core * 64 - half * 256
            keep = in_key <= reach
            edge = jnp.where(keep, edge, NEG_FILL)
            peak = highest(parts + [edge])
            weights = exponentials(parts, peak)
            weights.append(jnp.where(keep, exponentials([edge], peak)[0], 0.0))
            top[tile] = peak
            total[tile] = summed(weights)
            acc[tile] = gathered([span], [jnp.concatenate(weights, axis=0)])
            ready = later

        longest = jnp.zeros((8, 512), jnp.float32)
        for block in range(7):
            longest = jnp.maximum(longest, jnp.where(block < span, key_size[block], 0.0))
        longest = jnp.max(longest)

        def settle():
            fixed, width, lift = [], [], []
            for tile in range(4):
                bound = jnp.sqrt(q_size[turn, tile] * longest) * (1.004 * LOG2E / math.sqrt(HD))
                some = top[tile] > 0.5 * NEG_FILL
                low = jnp.where(some, top[tile], -bound)
                fixed.append(jnp.maximum(low, bound - 112.0))
                width.append(bound - low)
                lift.append(jnp.where(some, fixed[tile] - low, 0.0))
            calm = jnp.max(functools.reduce(jnp.maximum, width)) <= 212.0
            lifted = jnp.max(functools.reduce(jnp.maximum, lift)) > 0.0
            safe_now[0] = calm.astype(jnp.int32)

            @pl.when(jnp.logical_and(calm, lifted))
            def _():
                for tile in range(4):
                    scale = jnp.exp2(top[tile] - fixed[tile])
                    total[tile] = total[tile] * scale
                    acc[tile] = acc[tile] * scale[:1]

            @pl.when(calm)
            def _():
                for tile in range(4):
                    top[tile] = fixed[tile]

        settle()

        def sweep(blocks):
            units = [(tile, block, at) for block in blocks for tile in range(4) for at in range(0, 512, 512)]

            def unit_score(unit):
                tile, block, at = unit
                return lax.dot_general(
                    keys[block, at : at + 512, :],
                    q_all[tile * 512 : (tile + 1) * 512, :],
                    (((1,), (1,)), ((), ())),
                    preferred_element_type=jnp.float32,
                ) * (LOG2E / math.sqrt(HD))

            def unit_add(unit, weight):
                tile, block, at = unit
                acc[tile] += lax.dot_general(
                    values[block, at : at + 512, :],
                    weight,
                    (((0,), (0,)), ((), ())),
                    preferred_element_type=jnp.float32,
                )

            ready, waiting = unit_score(units[0]), None
            for index, unit in enumerate(units):
                later = unit_score(units[index + 1]) if index + 1 < len(units) else None
                weight = exponentials([ready], top[unit[0]])[0]
                total[unit[0]] += summed([weight])
                if waiting is not None:
                    unit_add(units[index - 1], waiting)
                waiting, ready = weight.astype(jnp.bfloat16), later
            unit_add(units[-1], waiting)

        def exact_sweep(block):
            for tile in range(4):
                weights, scale = weigh(tile, [score(q_all, tile, block, 512)])
                add(tile, [block], weights, scale)

        @pl.loop(0, span // 2)
        def _(group):
            calm = safe_now[0]

            @pl.when(calm == 1)
            def _():
                sweep([group * 2 + i for i in range(2)])

            @pl.when(calm == 0)
            def _():
                for i in range(2):
                    exact_sweep(group * 2 + i)
                settle()

        @pl.when((span & 1) == 1)
        def _():
            calm = safe_now[0]

            @pl.when(calm == 1)
            def _():
                sweep([span - 1])

            @pl.when(calm == 0)
            def _():
                exact_sweep(span - 1)

        term = lax.broadcasted_iota(jnp.int32, (8, 512), 0)
        for tile in range(4):
            whole = jnp.sum(total[tile], axis=0, keepdims=True)
            some = whole > 0
            safe = jnp.where(some, whole, 1.0)
            normed = (acc[tile] * (1.0 / safe)).astype(jnp.bfloat16)
            stat = jnp.where(some, (top[tile] + jnp.log2(safe)) * LN2, NEG_FILL)
            coarse = stat.astype(jnp.bfloat16).astype(jnp.float32)
            middle = (stat - coarse).astype(jnp.bfloat16).astype(jnp.float32)
            fine = stat - coarse - middle
            terms = jnp.where(term == 0, coarse, jnp.where(term == 1, middle, fine))
            for part in range(2):
                cols = slice(part * 256, (part + 1) * 256)
                at = member * 8 + tile * 2 + part
                o_ref[at, :HD, :] = normed[:, cols]
                o_ref[at, HD:, :] = terms[:, cols].astype(jnp.bfloat16)


def attend(place, q_pieces, own, other):
    whole = pl.BlockSpec(memory_space=pltpu.VMEM)
    return pl.pallas_call(
        attend_body,
        out_shape=jax.ShapeDtypeStruct((16, DEPTH, 256), jnp.bfloat16),
        in_specs=[pl.BlockSpec(memory_space=pltpu.SMEM)] + [whole] * 4,
        out_specs=whole,
        scratch_shapes=[
            pltpu.VMEM((8, 512, HD), jnp.bfloat16),
            pltpu.VMEM((8, 512, HD), jnp.bfloat16),
            pltpu.VMEM((4, HD, 512), jnp.float32),
            pltpu.VMEM((4, 8, 512), jnp.float32),
            pltpu.VMEM((4, 8, 512), jnp.float32),
            pltpu.VMEM((7, 8, 512), jnp.float32),
            pltpu.SMEM((1,), jnp.int32),
        ],
        compiler_params=pltpu.CompilerParams(vmem_limit_bytes=32 * 2**20),
        cost_estimate=pl.CostEstimate(
            flops=36 * 4 * 512 * 512 * HD,
            bytes_accessed=4 * 2**20,
            transcendentals=36 * 512 * 512,
        ),
        name="attend",
    )(place, *q_pieces, own, other)


def merge_body(got_ref, out_ref, log_ref, mixed_ref, left):
    gives = []
    for block in range(2 * SIDES):
        sums = []
        for member in range(2):
            terms = got_ref[member, block, HD:, :].astype(jnp.float32)
            sums.append(terms[0:1] + terms[1:2] + terms[2:3])
        high = jnp.maximum(sums[0], sums[1])
        joint = high + jnp.log(jnp.exp(sums[0] - high) + jnp.exp(sums[1] - high))
        mixed = got_ref[0, block, :HD, :].astype(jnp.float32) * jnp.exp(sums[0] - joint) + (
            got_ref[1, block, :HD, :].astype(jnp.float32) * jnp.exp(sums[1] - joint)
        )
        for pair in range(2):
            rows = mixed[:, pair * HD : (pair + 1) * HD].T.astype(jnp.bfloat16)
            for head in range(2):
                place = block * HELD + pair * 2 + head
                mixed_ref[:, place * HD : (place + 1) * HD] = rows[head * 64 : (head + 1) * 64]
                at = (pair * 2 + head) * 64
                log_ref[place : place + 1, :] = joint[:, at : at + 64]
        cols = slice(block * HELD * HD, (block + 1) * HELD * HD)
        gives.append(
            pltpu.make_async_copy(mixed_ref.at[:, cols], out_ref.at[:, cols], left.at[block])
        )
        gives[-1].start()
    for give in gives:
        give.wait()


def merge(got):
    whole = pl.BlockSpec(memory_space=pltpu.VMEM)
    return pl.pallas_call(
        merge_body,
        out_shape=(
            jax.ShapeDtypeStruct((64, HQ * HD), jnp.bfloat16),
            jax.ShapeDtypeStruct((HQ, 64), jnp.float32),
        ),
        in_specs=[whole],
        out_specs=(pl.BlockSpec(memory_space=pl.ANY), whole),
        scratch_shapes=[
            pltpu.VMEM((64, HQ * HD), jnp.bfloat16),
            pltpu.SemaphoreType.DMA((2 * SIDES,)),
        ],
        compiler_params=pltpu.CompilerParams(vmem_limit_bytes=8 * 2**20),
        name="merge",
    )(got.reshape(2, 2 * SIDES, DEPTH, 256))


def per_device(queries, key_states, value_states):
    row = lax.axis_index("qrow")
    column = lax.axis_index("kcol")
    place = jnp.stack([row, column])

    couple = swapped(queries, 96)
    own = lax.all_to_all(
        pack(key_states, value_states), EVERY, 0, 0, axis_index_groups=KEY_GROUPS
    )

    kept, given = split(place, queries, couple)
    taken = swapped(given, 1)

    arranged = arrange(place, kept, taken)
    own, arranged = lax.optimization_barrier((own, arranged))
    other = swapped(own, 1)
    partial = attend(place, arranged, own, other)
    got = lax.all_to_all(partial, EVERY, 0, 0, axis_index_groups=OUTPUT_GROUPS)
    mixed, logs = merge(got)
    return (mixed, logs.T)


def solution(mesh):
    placed = (P("qrow", "kcol"), P(("kcol", "qrow"), None), P(("kcol", "qrow"), None))
    return jax.shard_map(
        per_device,
        mesh=mesh,
        in_specs=placed,
        out_specs=(P(("qrow", "kcol"), None), P(("qrow", "kcol"), None)),
        check_vma=False,
    )
```

```python
import functools
import math

import jax
import jax.numpy as jnp
from jax import lax
from jax.experimental import pallas as pl
from jax.experimental.pallas import tpu as pltpu
from jax.sharding import PartitionSpec as P

HQ = 32
KVH = 4
HD = 128
GROUP = 8
EVERY = ("qrow", "kcol")
SPANS = 8
DEVICES = 128
SIDES = 4

NEG_FILL = -1e30
LOG2E = math.log2(math.e)
LN2 = math.log(2.0)
HELD = 4
DEPTH = 136


def device_at(span, side, slot):
    return span * 16 + side * 4 + slot


KEY_GROUPS = [
    [
        device_at(half * 4 + near, side, xh * 2 + core)
        for near in range(4)
        for xh in range(2)
        for side in range(SIDES)
    ]
    for half in range(2)
    for core in range(2)
]
OUTPUT_GROUPS = [
    [
        device_at(span, side, xh * 2 + core)
        for span in (low, low ^ 6)
        for side in range(SIDES)
        for xh in range(2)
    ]
    for low in range(SPANS // 2)
    for core in range(2)
]


def swapped(array, bits):
    return lax.ppermute(array, EVERY, [(i, i ^ bits) for i in range(DEVICES)])


def pack_body(key_ref, value_ref, out_ref):
    for side in range(SIDES):
        cols = slice(side * HD, (side + 1) * HD)
        for copy in range(8):
            out_ref[copy * SIDES + side, :, :HD] = key_ref[:, cols]
            out_ref[copy * SIDES + side, :, HD:] = value_ref[:, cols]


def pack(key_states, value_states):
    whole = pl.BlockSpec(memory_space=pltpu.VMEM)
    return pl.pallas_call(
        pack_body,
        out_shape=jax.ShapeDtypeStruct((32, 64, 2 * HD), jnp.bfloat16),
        in_specs=[whole, whole],
        out_specs=whole,
        name="pack",
    )(key_states, value_states)


def split_body(place, own_ref, couple_ref, kept_ref, given_ref):
    core = place[1] & 1
    for shift, out_ref in ((0, kept_ref), (1, given_ref)):
        for turn, ref in enumerate((own_ref, couple_ref)):
            for piece in range(8):
                at = pl.multiple_of(piece * 128 + (core ^ shift) * 64, 64)
                out_ref[turn, piece] = ref[pl.ds(at, 64), :]


def split(place, own, couple):
    whole = pl.BlockSpec(memory_space=pltpu.VMEM)
    return pl.pallas_call(
        split_body,
        out_shape=[jax.ShapeDtypeStruct((2, 8, 64, 2 * HD), jnp.bfloat16)] * 2,
        in_specs=[pl.BlockSpec(memory_space=pltpu.SMEM), whole, whole],
        out_specs=[whole] * 2,
        cost_estimate=pl.CostEstimate(
            flops=2 * 10**10, bytes_accessed=2**21, transcendentals=0
        ),
        compiler_params=pltpu.CompilerParams(vmem_limit_bytes=8 * 2**20),
        name="split",
    )(place, own, couple)


def grouped(scores):
    return scores.reshape(scores.shape[0] // 8, 8, scores.shape[1])


def highest(parts):
    high = functools.reduce(jnp.maximum, [jnp.max(grouped(part), axis=0) for part in parts])
    return jnp.broadcast_to(jnp.max(high, axis=0, keepdims=True), high.shape)


def exponentials(parts, peak):
    return [
        jnp.exp2(grouped(part) - peak[None]).reshape(part.shape) for part in parts
    ]


def summed(parts):
    return functools.reduce(jnp.add, [jnp.sum(grouped(part), axis=0) for part in parts])


def lengths(vectors):
    return lax.dot_general(
        jnp.ones((8, HD), jnp.bfloat16),
        vectors * vectors,
        (((1,), (1,)), ((), ())),
        preferred_element_type=jnp.float32,
    )


def arrange_body(place, kept_ref, taken_ref, q_both, q_size):
    core = place[1] & 1
    for turn in range(2):
        for shift, ref in ((0, kept_ref), (1, taken_ref)):
            for piece in range(8):
                for head in range(2):
                    at = piece * 256 + (core ^ shift) * 128 + head * 64
                    q_both[turn, pl.ds(pl.multiple_of(at, 64), 64), :] = ref[
                        turn, piece, :, head * HD : (head + 1) * HD
                    ]
        for tile in range(4):
            q_size[turn, tile] = lengths(q_both[turn, tile * 512 : (tile + 1) * 512, :])


def arrange(place, kept, taken):
    whole = pl.BlockSpec(memory_space=pltpu.VMEM)
    return pl.pallas_call(
        arrange_body,
        out_shape=[
            jax.ShapeDtypeStruct((2, 2048, HD), jnp.bfloat16),
            jax.ShapeDtypeStruct((2, 4, 8, 512), jnp.float32),
        ],
        in_specs=[pl.BlockSpec(memory_space=pltpu.SMEM), whole, whole],
        out_specs=[whole, whole],
        compiler_params=pltpu.CompilerParams(vmem_limit_bytes=8 * 2**20),
        name="arrange",
    )(place, kept, taken)


def attend_body(place, *refs):
    q_both, q_size, own_ref, other_ref, o_ref = refs[:5]
    keys, values, acc, top, total, key_size, safe_now = refs[5:]
    row, column = place[0], place[1]
    half, core = row >> 2, column & 1

    for ref, part in ((own_ref, core), (other_ref, 1 - core)):
        for block in range(8):
            side, xh = block // 2, block % 2
            for near in range(4):
                held = pl.ds(pl.multiple_of(part * 256 + near * 64, 64), 64)
                piece = (near * 2 + xh) * SIDES + side
                keys[block, held, :] = ref[piece, :, :HD]
                values[block, held, :] = ref[piece, :, HD:]

    for block in range(7):
        key_size[block] = lengths(keys[block])

    def score(q_all, tile, block, width):
        return lax.dot_general(
            keys[block, :width, :],
            q_all[tile * 512 : (tile + 1) * 512, :],
            (((1,), (1,)), ((), ())),
            preferred_element_type=jnp.float32,
        ) * (LOG2E / math.sqrt(HD))

    def gathered(blocks, weights):
        return sum(
            lax.dot_general(
                values[block, : weight.shape[0], :],
                weight.astype(jnp.bfloat16),
                (((0,), (0,)), ((), ())),
                preferred_element_type=jnp.float32,
            )
            for block, weight in zip(blocks, weights)
        )

    def weigh(tile, parts):
        old = top[tile]
        new = jnp.maximum(old, highest(parts))
        scale = jnp.exp2(old - new)
        weights = exponentials(parts, new)
        top[tile] = new
        total[tile] = total[tile] * scale + summed(weights)
        return weights, scale

    def add(tile, blocks, weights, scale):
        acc[tile] = acc[tile] * scale[:1] + gathered(blocks, weights)

    in_key = lax.broadcasted_iota(jnp.int32, (256, 512), 0)
    in_tile = lax.broadcasted_iota(jnp.int32, (256, 512), 1)
    in_row = (in_tile >> 8) * 128 + (in_tile & 63)
    for turn in range(2):
        span = row if turn == 0 else row ^ 6
        member = (row >> 2) ^ turn
        q_all = q_both.at[turn]

        def ahead(tile):
            return score(q_all, tile, span, 256 if tile < 2 else 512)

        order = (3, 2, 1, 0)
        ready = ahead(order[0])
        for at, tile in enumerate(order):
            later = ahead(order[at + 1]) if at < 3 else None
            edge, parts = ready[-256:], [ready[:256]] if tile >= 2 else []
            reach = in_row + (tile % 2) * 256 + core * 64 - half * 256
            keep = in_key <= reach
            edge = jnp.where(keep, edge, NEG_FILL)
            peak = highest(parts + [edge])
            weights = exponentials(parts, peak)
            weights.append(jnp.where(keep, exponentials([edge], peak)[0], 0.0))
            top[tile] = peak
            total[tile] = summed(weights)
            acc[tile] = gathered([span], [jnp.concatenate(weights, axis=0)])
            ready = later

        longest = jnp.zeros((8, 512), jnp.float32)
        for block in range(7):
            longest = jnp.maximum(longest, jnp.where(block < span, key_size[block], 0.0))
        longest = jnp.max(longest)

        def settle():
            fixed, width, lift = [], [], []
            for tile in range(4):
                bound = jnp.sqrt(q_size[turn, tile] * longest) * (1.004 * LOG2E / math.sqrt(HD))
                some = top[tile] > 0.5 * NEG_FILL
                low = jnp.where(some, top[tile], -bound)
                fixed.append(jnp.maximum(low, bound - 112.0))
                width.append(bound - low)
                lift.append(jnp.where(some, fixed[tile] - low, 0.0))
            calm = jnp.max(functools.reduce(jnp.maximum, width)) <= 212.0
            lifted = jnp.max(functools.reduce(jnp.maximum, lift)) > 0.0
            safe_now[0] = calm.astype(jnp.int32)

            @pl.when(jnp.logical_and(calm, lifted))
            def _():
                for tile in range(4):
                    scale = jnp.exp2(top[tile] - fixed[tile])
                    total[tile] = total[tile] * scale
                    acc[tile] = acc[tile] * scale[:1]

            @pl.when(calm)
            def _():
                for tile in range(4):
                    top[tile] = fixed[tile]

        settle()

        def sweep(blocks):
            units = [(tile, block, at) for block in blocks for tile in range(4) for at in range(0, 512, 512)]

            def unit_score(unit):
                tile, block, at = unit
                return lax.dot_general(
                    keys[block, at : at + 512, :],
                    q_all[tile * 512 : (tile + 1) * 512, :],
                    (((1,), (1,)), ((), ())),
                    preferred_element_type=jnp.float32,
                ) * (LOG2E / math.sqrt(HD))

            def unit_add(unit, weight):
                tile, block, at = unit
                acc[tile] += lax.dot_general(
                    values[block, at : at + 512, :],
                    weight,
                    (((0,), (0,)), ((), ())),
                    preferred_element_type=jnp.float32,
                )

            ready, waiting = unit_score(units[0]), None
            for index, unit in enumerate(units):
                later = unit_score(units[index + 1]) if index + 1 < len(units) else None
                weight = exponentials([ready], top[unit[0]])[0]
                total[unit[0]] += summed([weight])
                if waiting is not None:
                    unit_add(units[index - 1], waiting)
                waiting, ready = weight.astype(jnp.bfloat16), later
            unit_add(units[-1], waiting)

        def exact_sweep(block):
            for tile in range(4):
                weights, scale = weigh(tile, [score(q_all, tile, block, 512)])
                add(tile, [block], weights, scale)

        @pl.loop(0, span // 2)
        def _(group):
            calm = safe_now[0]

            @pl.when(calm == 1)
            def _():
                sweep([group * 2 + i for i in range(2)])

            @pl.when(calm == 0)
            def _():
                for i in range(2):
                    exact_sweep(group * 2 + i)
                settle()

        @pl.when((span & 1) == 1)
        def _():
            calm = safe_now[0]

            @pl.when(calm == 1)
            def _():
                sweep([span - 1])

            @pl.when(calm == 0)
            def _():
                exact_sweep(span - 1)

        term = lax.broadcasted_iota(jnp.int32, (8, 512), 0)
        for tile in range(4):
            whole = jnp.sum(total[tile], axis=0, keepdims=True)
            some = whole > 0
            safe = jnp.where(some, whole, 1.0)
            normed = (acc[tile] * (1.0 / safe)).astype(jnp.bfloat16)
            stat = jnp.where(some, (top[tile] + jnp.log2(safe)) * LN2, NEG_FILL)
            coarse = stat.astype(jnp.bfloat16).astype(jnp.float32)
            middle = (stat - coarse).astype(jnp.bfloat16).astype(jnp.float32)
            fine = stat - coarse - middle
            terms = jnp.where(term == 0, coarse, jnp.where(term == 1, middle, fine))
            for part in range(2):
                cols = slice(part * 256, (part + 1) * 256)
                at = member * 8 + tile * 2 + part
                o_ref[at, :HD, :] = normed[:, cols]
                o_ref[at, HD:, :] = terms[:, cols].astype(jnp.bfloat16)


def attend(place, q_pieces, own, other):
    whole = pl.BlockSpec(memory_space=pltpu.VMEM)
    return pl.pallas_call(
        attend_body,
        out_shape=jax.ShapeDtypeStruct((16, DEPTH, 256), jnp.bfloat16),
        in_specs=[pl.BlockSpec(memory_space=pltpu.SMEM)] + [whole] * 4,
        out_specs=whole,
        scratch_shapes=[
            pltpu.VMEM((8, 512, HD), jnp.bfloat16),
            pltpu.VMEM((8, 512, HD), jnp.bfloat16),
            pltpu.VMEM((4, HD, 512), jnp.float32),
            pltpu.VMEM((4, 8, 512), jnp.float32),
            pltpu.VMEM((4, 8, 512), jnp.float32),
            pltpu.VMEM((7, 8, 512), jnp.float32),
            pltpu.SMEM((1,), jnp.int32),
        ],
        compiler_params=pltpu.CompilerParams(vmem_limit_bytes=32 * 2**20),
        cost_estimate=pl.CostEstimate(
            flops=36 * 4 * 512 * 512 * HD,
            bytes_accessed=4 * 2**20,
            transcendentals=36 * 512 * 512,
        ),
        name="attend",
    )(place, *q_pieces, own, other)


def merge_body(got_ref, mixed_ref, log_ref):
    for block in range(2 * SIDES):
        sums = []
        for member in range(2):
            terms = got_ref[member, block, HD:, :].astype(jnp.float32)
            sums.append(terms[0:1] + terms[1:2] + terms[2:3])
        high = jnp.maximum(sums[0], sums[1])
        joint = high + jnp.log(jnp.exp(sums[0] - high) + jnp.exp(sums[1] - high))
        mixed = got_ref[0, block, :HD, :].astype(jnp.float32) * jnp.exp(sums[0] - joint) + (
            got_ref[1, block, :HD, :].astype(jnp.float32) * jnp.exp(sums[1] - joint)
        )
        for pair in range(2):
            rows = mixed[:, pair * HD : (pair + 1) * HD].T.astype(jnp.bfloat16)
            for head in range(2):
                place = block * HELD + pair * 2 + head
                mixed_ref[:, place * HD : (place + 1) * HD] = rows[head * 64 : (head + 1) * 64]
                at = (pair * 2 + head) * 64
                log_ref[place : place + 1, :] = joint[:, at : at + 64]


def merge(got):
    whole = pl.BlockSpec(memory_space=pltpu.VMEM)
    return pl.pallas_call(
        merge_body,
        out_shape=(
            jax.ShapeDtypeStruct((64, HQ * HD), jnp.bfloat16),
            jax.ShapeDtypeStruct((HQ, 64), jnp.float32),
        ),
        in_specs=[whole],
        out_specs=(whole, whole),
        compiler_params=pltpu.CompilerParams(vmem_limit_bytes=8 * 2**20),
        name="merge",
    )(got.reshape(2, 2 * SIDES, DEPTH, 256))


def per_device(queries, key_states, value_states):
    row = lax.axis_index("qrow")
    column = lax.axis_index("kcol")
    place = jnp.stack([row, column])

    couple = swapped(queries, 96)
    own = lax.all_to_all(
        pack(key_states, value_states), EVERY, 0, 0, axis_index_groups=KEY_GROUPS
    )

    kept, given = split(place, queries, couple)
    taken = swapped(given, 1)

    arranged = arrange(place, kept, taken)
    own, arranged = lax.optimization_barrier((own, arranged))
    other = swapped(own, 1)
    partial = attend(place, arranged, own, other)
    got = lax.all_to_all(partial, EVERY, 0, 0, axis_index_groups=OUTPUT_GROUPS)
    mixed, logs = merge(got)
    return (mixed, logs.T)


def solution(mesh):
    placed = (P("qrow", "kcol"), P(("kcol", "qrow"), None), P(("kcol", "qrow"), None))
    return jax.shard_map(
        per_device,
        mesh=mesh,
        in_specs=placed,
        out_specs=(P(("qrow", "kcol"), None), P(("qrow", "kcol"), None)),
        check_vma=False,
    )
```
